32 devices in a mesh: blk: 8 (over z, y), grp: 4 (over x, core).
Axes of the slice: x: 2, y: 2, z: 4, core: 2. Of those that a mesh axis runs over, the one named last changes fastest.
Arguments:
- features: bfloat16 [4096, 602], P(('blk', 'grp')), may hold values from -6 to 6
- adjacency: bfloat16 [4096, 4096], P(('blk', 'grp')), may hold values from -0.125 to 0.125
- tile_mask: int32 [32, 32], P(('blk', 'grp')), may hold values from 0 to 1, as said below
- labels: int32 [4096], P(('blk', 'grp')), may hold values from 0 to 40
- train_mask: int32 [4096], P(('blk', 'grp')), may hold values from 0 to 1
- w_first: float32 [602, 256], replicated, may hold values from -0.25 to 0.25
- w_second: float32 [256, 256], replicated, may hold values from -0.375 to 0.375
- w_head: float32 [256, 41], replicated, may hold values from -0.375 to 0.375
- norm_params: float32 [4, 256], replicated, may hold values from 0.5 to 1.5
- head_bias: float32 [41], replicated, may hold values from -3 to 3
- m_first: float32 [602, 256], replicated, may hold values from -0.001953125 to 0.001953125
- m_second: float32 [256, 256], replicated, may hold values from -0.001953125 to 0.001953125
- m_head: float32 [256, 41], replicated, may hold values from -0.001953125 to 0.001953125
- m_norms: float32 [4, 256], replicated, may hold values from -0.00390625 to 0.00390625
- m_bias: float32 [41], replicated, may hold values from -0.00390625 to 0.00390625
- v_first: float32 [602, 256], replicated, may hold values from 9.765625e-09 to 3.90625e-08
- v_second: float32 [256, 256], replicated, may hold values from 9.765625e-09 to 3.90625e-08
- v_head: float32 [256, 41], replicated, may hold values from 9.765625e-09 to 3.90625e-08
- v_norms: float32 [4, 256], replicated, may hold values from 3.90625e-08 to 1.5625e-07
- v_bias: float32 [41], replicated, may hold values from 3.90625e-08 to 1.5625e-07
Outputs:
- loss_sum: float32 [], replicated
- train_count: float32 [], replicated
- new_first: float32 [602, 256], replicated
- new_second: float32 [256, 256], replicated
- new_head: float32 [256, 41], replicated
- new_norms: float32 [4, 256], replicated
- new_bias: float32 [41], replicated
- first_m_first: float32 [602, 256], replicated
- first_m_second: float32 [256, 256], replicated
- first_m_head: float32 [256, 41], replicated
- first_m_norms: float32 [4, 256], replicated
- first_m_bias: float32 [41], replicated
- second_v_first: float32 [602, 256], replicated
- second_v_second: float32 [256, 256], replicated
- second_v_head: float32 [256, 41], replicated
- second_v_norms: float32 [4, 256], replicated
- second_v_bias: float32 [41], replicated
The draws below stay inside these ranges and needn't reach their ends.
Inputs may be any that keep to these rules, and one draw needn't show every extreme that they name: `tile_mask`: every diagonal tile is set.
All inputs are finite; a program needn't handle non-finite values.
Results may differ from the reference program's by a relative error of at most 0.0083.
Values may be sent and summed in bfloat16 or wider, within the bound.
No kernel may reach another device: no remote copies, remote signals or barrier semaphores. Data moves between devices by JAX's collectives and lax.ppermute only.
A program may use at most 128 MiB of HBM per device.

```python
import math
import jax
import jax.numpy as jnp
from jax import lax

F_IN = 602
HID = 256
CLS = 41
TILE = 128
STEP = 10
NODES = 4096


def draw_tile_mask(key, part):
    key = jax.random.fold_in(key, 11)
    tiles = NODES // TILE
    rolls = jax.random.randint(key, (tiles, tiles), 0, 1000)
    row_index = jnp.arange(tiles, dtype=jnp.int32)[:, None]
    col_index = jnp.arange(tiles, dtype=jnp.int32)[None, :]
    limit = 250 + 500 * row_index // max(tiles - 1, 1)
    chosen = (rolls < limit) | (row_index == col_index)
    return jnp.where(chosen, 1, 0).astype(jnp.int32)


def draw_train_mask(key, part):
    key = jax.random.fold_in(key, 23)
    rolls = jax.random.randint(key, (NODES,), 0, 1000)
    node_index = jnp.arange(NODES, dtype=jnp.int32)
    limit = 300 + 600 * node_index // max(NODES - 1, 1)
    return jnp.where(rolls < limit, 1, 0).astype(jnp.int32)


def plant(entries, stream_key, least, largest):
    place = [jax.random.randint(jax.random.fold_in(stream_key, axis), (), 0, length) for axis, length in enumerate(entries.shape)]
    main_axis = entries.shape.index(max(entries.shape))
    neighbour = place[:main_axis] + [(place[main_axis] + 1) % entries.shape[main_axis]] + place[main_axis + 1:]
    return entries.at[tuple(place)].set(least).at[tuple(neighbour)].set(largest)


def steps_of(rng, dims, split, smallest, largest):
    def one(axis_at, shards_of):
        draws = jax.random.uniform(jax.random.fold_in(jax.random.fold_in(rng, 6), axis_at), (shards_of,), jnp.float32, smallest / len(split), largest / len(split))
        return jnp.repeat(jnp.exp(draws), dims[axis_at] // shards_of).reshape((-1,) + (1,) * (len(dims) - axis_at - 1))

    factor_of = one(*split[0])
    for cut in split[1:]:
        factor_of = factor_of * one(*cut)
    return factor_of


def gaussian(own_key, dims, scale, bound, cuts=(), kind=jnp.bfloat16):
    entries = scale * jax.random.normal(own_key, dims, jnp.float32)
    if cuts:
        entries = entries * steps_of(own_key, dims, cuts, -0.22, 0.18)
    return jnp.clip(entries, -bound, bound).astype(kind)


def setup_inputs(seed: int = 0) -> dict:
    splits = jax.random.split(jax.random.key(seed), 21)
    features = gaussian(splits[0], (NODES, F_IN), 1.0, 6.0, ((0, 32),))
    adjacency = gaussian(splits[1], (NODES, NODES), (NODES // 2) ** -0.5, 0.125, ((0, 32),))
    tile_mask = draw_tile_mask(jax.random.fold_in(splits[20], 71), 0)
    labels = plant(jax.random.randint(splits[3], (NODES,), 0, CLS), jax.random.fold_in(splits[3], 1), 0, CLS - 1).astype(jnp.int32)
    train_mask = draw_train_mask(jax.random.fold_in(splits[20], 71), 0)
    w_first = gaussian(splits[5], (F_IN, HID), F_IN ** -0.5, 0.25, (), jnp.float32)
    w_second = gaussian(splits[6], (HID, HID), HID ** -0.5, 0.375, (), jnp.float32)
    w_head = gaussian(splits[7], (HID, CLS), HID ** -0.5, 0.375, (), jnp.float32)
    norm_params = jnp.clip(1.0 + 0.1 * jax.random.normal(splits[8], (4, HID), jnp.float32), 0.5, 1.5)
    head_bias = gaussian(splits[9], (CLS,), 0.5, 3.0, (), jnp.float32)
    m_first = gaussian(splits[10], (F_IN, HID), (0.022 * NODES ** -0.5), 0.001953125, (), jnp.float32)
    m_second = gaussian(splits[11], (HID, HID), (0.022 * NODES ** -0.5), 0.001953125, (), jnp.float32)
    m_head = gaussian(splits[12], (HID, CLS), (0.022 * NODES ** -0.5), 0.001953125, (), jnp.float32)
    m_norms = gaussian(splits[13], (4, HID), (0.044 * NODES ** -0.5), 0.00390625, (), jnp.float32)
    m_bias = gaussian(splits[14], (CLS,), (0.044 * NODES ** -0.5), 0.00390625, (), jnp.float32)
    v_first = jnp.clip(jnp.exp(jax.random.uniform(splits[15], (F_IN, HID), jnp.float32, math.log(9.765624753299562e-09), math.log(3.906249901319825e-08))), 9.765624753299562e-09, 3.906249901319825e-08)
    v_second = jnp.clip(jnp.exp(jax.random.uniform(splits[16], (HID, HID), jnp.float32, math.log(9.765624753299562e-09), math.log(3.906249901319825e-08))), 9.765624753299562e-09, 3.906249901319825e-08)
    v_head = jnp.clip(jnp.exp(jax.random.uniform(splits[17], (HID, CLS), jnp.float32, math.log(9.765624753299562e-09), math.log(3.906249901319825e-08))), 9.765624753299562e-09, 3.906249901319825e-08)
    v_norms = jnp.clip(jnp.exp(jax.random.uniform(splits[18], (4, HID), jnp.float32, math.log(3.906249901319825e-08), math.log(1.56249996052793e-07))), 3.906249901319825e-08, 1.56249996052793e-07)
    v_bias = jnp.clip(jnp.exp(jax.random.uniform(splits[19], (CLS,), jnp.float32, math.log(3.906249901319825e-08), math.log(1.56249996052793e-07))), 3.906249901319825e-08, 1.56249996052793e-07)
    return {"features": features, "adjacency": adjacency, "tile_mask": tile_mask, "labels": labels, "train_mask": train_mask, "w_first": w_first, "w_second": w_second, "w_head": w_head, "norm_params": norm_params, "head_bias": head_bias, "m_first": m_first, "m_second": m_second, "m_head": m_head, "m_norms": m_norms, "m_bias": m_bias, "v_first": v_first, "v_second": v_second, "v_head": v_head, "v_norms": v_norms, "v_bias": v_bias}


EPS_NORM = 1e-05
EPS_ADAM = 1e-08
BETA_ONE = 0.9
BETA_TWO = 0.999
DECAY = 0.01
RATE_MATRIX = 0.03
RATE_SMALL = 0.3

@jax.custom_vjp
def low(v):
    return lax.optimization_barrier(v.astype(jnp.bfloat16)).astype(jnp.float32)

@jax.custom_vjp
def low_back(v):
    return v

def low_keep(v):
    return (low(v), None)

def low_pass(kept, grad):
    return (grad,)

def back_keep(v):
    return (v, None)

def back_low(kept, grad):
    return (low(grad),)
low.defvjp(low_keep, low_pass)
low_back.defvjp(back_keep, back_low)

def multiply(left, right):
    return jnp.dot(left, right, precision=lax.Precision.HIGHEST, preferred_element_type=jnp.float32)

def adamw(weight, gradient, first, second, rate):
    first_new = BETA_ONE * first + (1.0 - BETA_ONE) * gradient
    second_new = BETA_TWO * second + (1.0 - BETA_TWO) * gradient * gradient
    scaled = first_new / (1.0 - BETA_ONE ** STEP) / (jnp.sqrt(second_new / (1.0 - BETA_TWO ** STEP)) + EPS_ADAM)
    return (weight - rate * (scaled + DECAY * weight), first_new, second_new)

def reference(features, adjacency, tile_mask, labels, train_mask, w_first, w_second, w_head, norm_params, head_bias, m_first, m_second, m_head, m_norms, m_bias, v_first, v_second, v_head, v_norms, v_bias):
    keep = jnp.repeat(jnp.repeat(tile_mask, TILE, axis=0), TILE, axis=1).astype(jnp.float32)
    adjacent = adjacency.astype(jnp.float32) * keep
    inputs = features.astype(jnp.float32)
    weights_mask = train_mask.astype(jnp.float32)
    onehot = (labels[:, None] == jnp.arange(CLS, dtype=jnp.int32)[None, :]).astype(jnp.float32)

    def hidden_layer(values, matrix, gain_row, shift_row):
        projected = low(low_back(multiply(low(values), low(matrix))))
        summed = low_back(multiply(adjacent, projected))
        mean_value = lax.optimization_barrier(jnp.mean(summed, axis=0))
        centred = summed - mean_value
        variance = lax.optimization_barrier(jnp.mean(centred * centred, axis=0))
        normed = centred * lax.rsqrt(variance + EPS_NORM)
        return jax.nn.gelu(gain_row * normed + shift_row)

    def forward(params):
        first, second, head, norms, bias = params
        hidden_one = hidden_layer(inputs, first, norms[0], norms[1])
        hidden_two = hidden_layer(hidden_one, second, norms[2], norms[3])
        gathered = low(low_back(multiply(adjacent, low(hidden_two))))
        logits = low_back(multiply(gathered, low(head))) + bias
        log_probs = jax.nn.log_softmax(logits, axis=1)
        losses = -lax.optimization_barrier(jnp.sum(onehot * log_probs, axis=1))
        total_loss = jnp.sum(losses * weights_mask)
        count_total = jnp.sum(weights_mask)
        return (total_loss / count_total, (total_loss, count_total))
    params = (w_first, w_second, w_head, norm_params, head_bias)
    value, pullback, extra = jax.vjp(forward, params, has_aux=True)
    grads = pullback(jnp.ones_like(value))[0]
    firsts = (m_first, m_second, m_head, m_norms, m_bias)
    seconds = (v_first, v_second, v_head, v_norms, v_bias)
    rates = (RATE_MATRIX, RATE_MATRIX, RATE_MATRIX, RATE_SMALL, RATE_SMALL)
    updated = [adamw(params[i], grads[i], firsts[i], seconds[i], rates[i]) for i in range(5)]
    return (extra[0], extra[1], updated[0][0], updated[1][0], updated[2][0], updated[3][0], updated[4][0], updated[0][1], updated[1][1], updated[2][1], updated[3][1], updated[4][1], updated[0][2], updated[1][2], updated[2][2], updated[3][2], updated[4][2])
```

```python
import functools
import math

import jax
import jax.numpy as jnp
from jax import lax
from jax.experimental import pallas as pl
from jax.experimental.pallas import tpu as pltpu
from jax.sharding import Mesh
from jax.sharding import PartitionSpec as P

TILE = 128
STEP = 10
EPS_NORM = 1e-05
EPS_ADAM = 1e-08
BETA_ONE = 0.9
BETA_TWO = 0.999
DECAY = 0.01
RATE_MATRIX = 0.03
RATE_SMALL = 0.3

BF = jnp.bfloat16
F32 = jnp.float32
PLANE = ("y", "x", "c")
EVERY = ("z", "y", "x", "c")
LANES = 128
HEAD_ROWS = 48
EXTRA = 16
ROOT = math.sqrt(2.0 / math.pi)
BEND = 0.044715


def adamw(weight, gradient, first, second, rate):
    first_new = BETA_ONE * first + (1.0 - BETA_ONE) * gradient
    second_new = BETA_TWO * second + (1.0 - BETA_TWO) * gradient * gradient
    scaled = (
        first_new
        / (1.0 - BETA_ONE**STEP)
        / (jnp.sqrt(second_new / (1.0 - BETA_TWO**STEP)) + EPS_ADAM)
    )
    return (weight - rate * (scaled + DECAY * weight), first_new, second_new)


def dot(left, right):
    return jnp.dot(left, right, preferred_element_type=F32)


def dot_turned(left, right):
    return lax.dot_general(left, right, (((1,), (1,)), ((), ())), preferred_element_type=F32)


def shape(dims, kind=F32):
    return jax.ShapeDtypeStruct(dims, kind)


def run(body, outs, ins, scratch=(), flops=0, scalars=0):
    held = sum(math.prod(a.shape[:-1]) * max(a.shape[-1], LANES) * a.dtype.itemsize for a in (*ins, *outs))
    limit = min(60 << 20, 2 * held + (8 << 20))
    return pl.pallas_call(
        body,
        out_shape=tuple(outs),
        in_specs=[pl.BlockSpec(memory_space=pltpu.SMEM)] * scalars
        + [pl.BlockSpec(memory_space=pltpu.VMEM)] * (len(ins) - scalars),
        out_specs=tuple(pl.BlockSpec(memory_space=pltpu.VMEM) for unused in outs),
        scratch_shapes=list(scratch),
        compiler_params=pltpu.CompilerParams(vmem_limit_bytes=limit),
        cost_estimate=pl.CostEstimate(flops=flops, bytes_accessed=held, transcendentals=0),
    )(*ins)


def swap(block, mask):
    return lax.ppermute(block, PLANE, [(i, i ^ mask) for i in range(8)])


def pass_line(block, mask):
    return lax.ppermute(block, "z", [(i, i ^ mask) for i in range(4)])


def short_line():
    return lax.axis_size("z") == 4


def gather_all(block):
    if short_line():
        line = jnp.stack([block] + [pass_line(block, k) for k in range(1, 4)])
    else:
        line = lax.all_gather(block, "z", axis=0)
    half = jnp.concatenate([line] + [swap(line, 2 * k) for k in range(1, 4)])
    return half, swap(half, 1)


def arrange_kernel(mask_ref, values_ref, near_ref, far_ref):
    half = near_ref.shape[1] // TILE
    lines = half // 4
    here = 4 * lax.axis_index("y") + 2 * lax.axis_index("x") + lax.axis_index("c")
    level = lax.axis_index("z") if short_line() else 0

    for core, out_ref in ((0, near_ref), (1, far_ref)):

        def one(step, carry, core=core, out_ref=out_ref):
            place, height = step // lines, jnp.bitwise_xor(step % lines, level)
            source = height * 8 + jnp.bitwise_xor(place * 2 + core, here)
            keep = mask_ref[0, source].astype(F32).astype(BF)
            out_ref[:, pl.ds(pl.multiple_of(step * TILE, TILE), TILE)] = (
                values_ref[:, pl.ds(pl.multiple_of(source * TILE, TILE), TILE)] * keep
            )
            return carry

        lax.fori_loop(0, half, one, 0)


def centre_into(out_ref, summed):
    rows = summed.shape[0]
    centre = (jnp.sum(summed, axis=0, keepdims=True) / rows).astype(BF).astype(F32)
    out_ref[:rows, :] = (summed - centre).astype(BF)
    out_ref[rows:, :] = jnp.broadcast_to(centre, (EXTRA, summed.shape[1])).astype(BF)


def moments(refs, node_total):
    count, tall, width = refs[0].shape
    rows = tall - EXTRA
    pivot = refs[0][0, rows:, :].astype(F32)[:1]
    zero = jnp.zeros((8, width), F32)
    sums = (zero, zero)
    for ref in refs:

        def one(i, carry, ref=ref):
            total, square = carry
            value = ref[i, :rows, :].astype(F32).reshape(rows // 8, 8, width)
            part = jnp.sum(value, axis=0)
            away = ref[i, rows:, :].astype(F32)[:1] - pivot
            each = away * (rows // 8)
            return (
                total + part + each,
                square + jnp.sum(value * value, axis=0) + away * (2.0 * part + each),
            )

        sums = lax.fori_loop(0, count, one, sums)
    shift = jnp.sum(sums[0], axis=0, keepdims=True) / node_total
    variance = jnp.sum(sums[1], axis=0, keepdims=True) / node_total - shift * shift
    return pivot + shift, lax.rsqrt(jnp.maximum(variance, 0.0) + EPS_NORM)


def gelu_half(value):
    square = value * value
    bend = jnp.tanh(value * (ROOT + (ROOT * BEND) * square))
    return 0.5 + 0.5 * bend, bend, square


def gelu_slope(value, half, bend, square):
    return half + (0.5 * value) * (1.0 - bend * bend) * (ROOT + (3 * ROOT * BEND) * square)


def blocks_of(ref, i, pair, rows):
    parts = [
        (ref[i * pair + j, :rows, :].astype(F32), ref[i * pair + j, rows:, :].astype(F32)[:1])
        for j in range(pair)
    ]
    return parts


def columns(ref, i, width):
    return ref[:, pl.ds(pl.multiple_of(i * width, width), width)]


def split_sums(total):
    high = total.astype(BF).astype(F32)
    low = (total - high).astype(BF).astype(F32)
    return jnp.concatenate([high, low])


def joined(parts):
    parts = parts.astype(F32)
    return parts[: EXTRA // 2] + parts[EXTRA // 2 :]


def put_sums(out_ref, width, parts):
    out_ref[width:, :LANES] = parts.astype(BF)
    if out_ref.shape[1] > LANES:
        out_ref[width:, LANES:] = jnp.zeros((EXTRA, out_ref.shape[1] - LANES), BF)


def spread_into(send_ref, turned, far_ref):
    width = turned.shape[0]
    step = min(512, far_ref.shape[1])
    for i in range(far_ref.shape[1] // step):
        send_ref[:width, i * step : (i + 1) * step] = dot(
            turned, far_ref[:, i * step : (i + 1) * step]
        ).astype(BF)


def fold_core_kernel(summing, turned_ref, near_ref, got_ref, *refs):
    if summing:
        parts_ref, kept_ref, *piece_refs, out_parts_ref = refs
    else:
        kept_ref, *piece_refs = refs
    width = turned_ref.shape[0]
    piece = kept_ref.shape[1]
    step = min(512, piece)
    for k in range(4):
        for i in range(piece // step):
            at = k * piece + i * step
            value = dot(turned_ref[...], near_ref[:, at : at + step])
            value = value + got_ref[:width, at : at + step].astype(F32)
            if k == 0:
                kept_ref[:, i * step : (i + 1) * step] = value
            else:
                piece_refs[k - 1][:width, i * step : (i + 1) * step] = value.astype(BF)
    if summing:
        parts = split_sums(joined(parts_ref[...]) + joined(got_ref[width:, :LANES]))
        out_parts_ref[...] = parts
        for piece_ref in piece_refs:
            put_sums(piece_ref, width, parts)


def sum_four(own, got_refs, width, cols=slice(None)):
    got = [ref[:width, cols].astype(F32) for ref in got_refs]
    return (own + got[0]) + (got[1] + got[2])


def sum_parts(parts, got_refs, width):
    got = [joined(ref[width:, :LANES]) for ref in got_refs]
    return (joined(parts) + got[0]) + (got[1] + got[2])


def fold_plane_kernel(summing, short, own_ref, *refs):
    got_refs, refs = refs[:3], refs[3:]
    width = own_ref.shape[0]
    if summing:
        parts = split_sums(sum_parts(refs[0][...], got_refs, width))
        refs = refs[1:]
    if not short:
        refs[0][...] = sum_four(own_ref[...], got_refs, width)
        if summing:
            refs[1][...] = parts
        return
    kept_ref, *piece_refs = refs[:4]
    for k in range(4):
        cols = slice(k * LANES, (k + 1) * LANES)
        value = sum_four(own_ref[:, cols], got_refs, width, cols)
        if k == 0:
            kept_ref[...] = value
        else:
            piece_refs[k - 1][:width, :] = value.astype(BF)
            if summing:
                put_sums(piece_refs[k - 1], width, parts)
    if summing:
        refs[4][...] = parts


def spread_back(turned, send, near, parts):
    width = turned.shape[0]
    tall = send.shape[0]
    piece = near.shape[1] // 4
    summing = parts is not None
    got = swap(send, 1)
    outs = [shape((width, piece))] + [shape((tall, piece), BF)] * 3
    ins = [turned, near, got] + [parts] * summing
    outs += [shape((EXTRA, LANES))] * summing
    own, *rest = run(
        functools.partial(fold_core_kernel, summing), outs, ins, flops=2 * width * LANES * piece * 4
    )
    pieces, parts = rest[:3], rest[3:]
    got = [swap(pieces[k - 1], 2 * k) for k in range(1, 4)]
    short = short_line()
    if short:
        outs = [shape((width, LANES))] + [shape((tall, LANES), BF)] * 3
    else:
        outs = [shape((width, piece))]
    outs += [shape((EXTRA, LANES))] * summing
    folded = run(functools.partial(fold_plane_kernel, summing, short), outs, [own, *got, *parts])
    if short:
        own, *rest = folded
        got = [pass_line(rest[k - 1], k) for k in range(1, 4)]
        return own, got, rest[3:]
    total = lax.psum_scatter(folded[0], "z", scatter_dimension=1, tiled=True)
    if not summing:
        return total, [], []
    return total, [], [lax.psum(folded[1][: EXTRA // 2] + folded[1][EXTRA // 2 :], "z")]


def line_sum(own_ref, got_refs, parts_refs):
    width = own_ref.shape[0]
    if got_refs:
        total = sum_four(own_ref[...], got_refs, width)
        sums = sum_parts(parts_refs[0][...], got_refs, width) if parts_refs else None
        return total, sums
    return own_ref[...], parts_refs[0][...] if parts_refs else None


def wide(sums, row):
    return jnp.concatenate([sums[row : row + 1], sums[row + 1 : row + 2]], axis=1)


def put_wide(ref, row, value):
    ref[row : row + 1, :] = value[:, :LANES]
    ref[row + 1 : row + 2, :] = value[:, LANES:]


def layer_kernel(node_total, layer, near_ref, far_ref, low_ref, norm_ref, half_ref, other_ref, out_ref, stats_ref):
    refs = (half_ref, other_ref)
    count, tall, width = half_ref.shape
    rows = tall - EXTRA
    mean_value, inverse = moments(refs, node_total)
    stats_ref[0:1, :] = mean_value
    stats_ref[1:2, :] = inverse
    scale = norm_ref[2 * layer : 2 * layer + 1, :] * inverse
    start = norm_ref[2 * layer + 1 : 2 * layer + 2, :] - mean_value * scale
    total = jnp.zeros((rows, low_ref.shape[1]), F32)
    for ref, adjacent_ref in ((half_ref, near_ref), (other_ref, far_ref)):

        def one(i, total, ref=ref, adjacent_ref=adjacent_ref):
            hidden = []
            for value, centre in blocks_of(ref, i, 2, rows):
                value = value * scale + (start + centre * scale)
                hidden.append((value * gelu_half(value)[0]).astype(BF))
            projected = dot(jnp.concatenate(hidden), low_ref[...]).astype(BF)
            return total + dot(columns(adjacent_ref, i, 2 * rows), projected)

        total = lax.fori_loop(0, count // 2, one, total, unroll=2)
    centre_into(out_ref, total)


def slopes_kernel(layer, near_ref, far_ref, norm_ref, half_ref, other_ref, stats_ref, out_ref):
    count, tall, width = half_ref.shape
    rows = tall - EXTRA
    mean_value, inverse = stats_ref[0:1, :], stats_ref[1:2, :]
    gain = norm_ref[2 * layer : 2 * layer + 1, :]
    offset = norm_ref[2 * layer + 1 : 2 * layer + 2, :]
    out_ref[...] = jnp.zeros(out_ref.shape, F32)
    for ref, adjacent_ref in ((half_ref, near_ref), (other_ref, far_ref)):

        def one(i, carry, ref=ref, adjacent_ref=adjacent_ref):
            slopes = []
            for value, centre in blocks_of(ref, i, 2, rows):
                normed = value * inverse + (centre - mean_value) * inverse
                value = gain * normed + offset
                slope = gelu_slope(value, *gelu_half(value))
                slopes.append(jnp.concatenate([slope.astype(BF), (slope * normed).astype(BF)], axis=1))
            out_ref[...] += dot(columns(adjacent_ref, i, 2 * rows), jnp.concatenate(slopes))
            return carry

        lax.fori_loop(0, count // 2, one, 0, unroll=2)


def head_kernel(
    node_total,
    classes,
    near_ref,
    far_ref,
    low_ref,
    norm_ref,
    bias_ref,
    label_ref,
    mask_ref,
    half_ref,
    other_ref,
    send_ref,
    turned_ref,
    parts_ref,
    stats_ref,
    total_ref,
    sums_ref,
):
    refs = (half_ref, other_ref)
    count, tall, width = half_ref.shape
    rows = tall - EXTRA
    mean_value, inverse = moments(refs, node_total)
    stats_ref[0:1, :] = mean_value
    stats_ref[1:2, :] = inverse
    gain, offset = norm_ref[2:3, :], norm_ref[3:4, :]
    total_ref[...] = jnp.zeros(total_ref.shape, F32)
    for ref, adjacent_ref in ((half_ref, near_ref), (other_ref, far_ref)):

        def one(i, carry, ref=ref, adjacent_ref=adjacent_ref):
            hidden, slopes = [], []
            for value, centre in blocks_of(ref, i, 2, rows):
                normed = value * inverse + (centre - mean_value) * inverse
                value = gain * normed + offset
                half, bend, square = gelu_half(value)
                slope = gelu_slope(value, half, bend, square)
                hidden.append((value * half).astype(BF))
                slopes.append(jnp.concatenate([slope.astype(BF), (slope * normed).astype(BF)], axis=1))
            headed = dot(jnp.concatenate(hidden), low_ref[...]).astype(BF)
            both = jnp.concatenate([headed, jnp.concatenate(slopes)], axis=1)
            total_ref[...] += dot(columns(adjacent_ref, i, 2 * rows), both)
            return carry

        lax.fori_loop(0, count // 2, one, 0, unroll=2)

    lane = lax.broadcasted_iota(jnp.int32, (rows, LANES), 1)
    logits = jnp.where(lane < classes, total_ref[:, :LANES] + bias_ref[...], -1e30)
    logits = logits - jnp.max(logits, axis=1, keepdims=True)
    raised = jnp.exp(logits)
    whole = jnp.sum(raised, axis=1, keepdims=True)
    onehot = jnp.where(lane == label_ref[...], 1.0, 0.0)
    weight = mask_ref[...].astype(F32)
    losses = jnp.log(whole) - jnp.sum(onehot * logits, axis=1, keepdims=True)
    d_logits = (raised / whole - onehot) * weight
    d_low = d_logits.astype(BF)
    d_wide = dot_turned(d_low, low_ref[...])
    put_wide(sums_ref, 0, jnp.sum(d_wide * total_ref[:, LANES : LANES + width], axis=0, keepdims=True))
    put_wide(sums_ref, 2, jnp.sum(d_wide * total_ref[:, LANES + width :], axis=0, keepdims=True))
    sums_ref[4:5, :] = jnp.sum(d_logits, axis=0, keepdims=True)
    first = lax.broadcasted_iota(jnp.int32, (rows, LANES), 1) == 0
    sums_ref[5:6, :] = jnp.sum(jnp.where(first, losses * weight, weight), axis=0, keepdims=True)
    sums_ref[6:8, :] = jnp.zeros((2, LANES), F32)
    parts = split_sums(sums_ref[...])
    parts_ref[...] = parts
    turned = d_logits.T[:HEAD_ROWS].astype(BF)
    turned_ref[...] = turned
    spread_into(send_ref, turned, far_ref)
    put_sums(send_ref, HEAD_ROWS, parts)


def backward_norm(d_hidden, own_ref, stats_ref, norm_ref, layer, shift_grad, gain_grad, node_total):
    rows = own_ref.shape[0] - EXTRA
    mean_value, inverse = stats_ref[0:1, :], stats_ref[1:2, :]
    gain = norm_ref[2 * layer : 2 * layer + 1, :]
    centre = own_ref[rows:, :].astype(F32)[:1]
    normed = own_ref[:rows, :].astype(F32) * inverse + (centre - mean_value) * inverse
    value = gain * normed + norm_ref[2 * layer + 1 : 2 * layer + 2, :]
    half, bend, square = gelu_half(value)
    d_pre = d_hidden * gelu_slope(value, half, bend, square)
    d_summed = (gain * inverse) * (d_pre - (shift_grad + normed * gain_grad) / node_total)
    return d_summed, value * half


def second_kernel(node_total, n_got, *refs):
    own_ref, got_refs, refs = refs[0], refs[1 : 1 + n_got], refs[1 + n_got :]
    (in_parts_ref, far_ref, head_ref, low_ref, norm_ref, summed_ref, stats_ref, slopes_ref) = refs[:8]
    send_ref, turned_ref, parts_ref, grad_ref, out_ref, sums_ref = refs[8:]
    headed, sums = line_sum(own_ref, got_refs, [in_parts_ref])
    rows = headed.shape[1]
    each = 1.0 / sums[5:6, 1:2]
    headed = headed * each
    put_row = lax.broadcasted_iota(jnp.int32, sums.shape, 0)
    out_ref[...] = jnp.where(put_row == 5, sums, sums * each)
    turned_back = jnp.concatenate([headed, jnp.zeros((LANES - HEAD_ROWS, rows), F32)]).T
    d_hidden = dot_turned(turned_back.astype(BF), head_ref[...])
    d_summed, hidden = backward_norm(
        d_hidden, summed_ref, stats_ref, norm_ref, 1, wide(sums, 0) * each, wide(sums, 2) * each, node_total
    )
    grad_ref[...] = dot(headed.astype(BF), hidden.astype(BF))
    d_low = d_summed.astype(BF)
    d_wide = dot_turned(d_low, low_ref[...])
    width = d_wide.shape[1]
    put_wide(sums_ref, 0, jnp.sum(d_wide * slopes_ref[:, :width], axis=0, keepdims=True))
    put_wide(sums_ref, 2, jnp.sum(d_wide * slopes_ref[:, width:], axis=0, keepdims=True))
    sums_ref[4:8, :] = jnp.zeros((4, LANES), F32)
    parts = split_sums(sums_ref[...])
    parts_ref[...] = parts
    turned = d_summed.T.astype(BF)
    turned_ref[...] = turned
    spread_into(send_ref, turned, far_ref)
    put_sums(send_ref, width, parts)


def first_kernel(node_total, n_got, *refs):
    own_ref, got_refs, refs = refs[0], refs[1 : 1 + n_got], refs[1 + n_got :]
    in_parts_ref, far_ref, low_ref, norm_ref, summed_ref, stats_ref = refs[:6]
    send_ref, turned_ref, grad_ref, out_ref = refs[6:]
    d_projected, sums = line_sum(own_ref, got_refs, [in_parts_ref])
    out_ref[...] = sums
    d_projected = d_projected.T.astype(BF)
    d_hidden = dot_turned(d_projected, low_ref[...])
    d_summed, hidden = backward_norm(
        d_hidden, summed_ref, stats_ref, norm_ref, 0, wide(sums, 0), wide(sums, 2), node_total
    )
    turned = d_summed.T.astype(BF)
    turned_ref[...] = turned
    spread_into(send_ref, turned, far_ref)
    grad_ref[...] = dot(hidden.T.astype(BF), d_projected)


def pile_kernel(n_got, *refs):
    own_ref, got_refs, refs = refs[0], refs[1 : 1 + n_got], refs[1 + n_got :]
    inputs_ref, second_ref, head_ref, away_ref, kept_ref, pile_ref = refs
    d_projected = line_sum(own_ref, got_refs, [])[0].T.astype(BF)
    at = inputs_ref.shape[0]
    pile_ref[:at, :] = dot(inputs_ref[...], d_projected)
    pile_ref[at : at + second_ref.shape[0], :] = second_ref[...]
    at += second_ref.shape[0]
    pile_ref[at : at + HEAD_ROWS, :] = head_ref[...]
    at += HEAD_ROWS
    pile_ref[at:, :] = jnp.zeros((pile_ref.shape[0] - at, pile_ref.shape[1]), F32)
    half = away_ref.shape[0]
    core = lax.axis_index("c")
    away_ref[...] = pile_ref[pl.ds(pl.multiple_of((1 - core) * half, half), half), :].astype(BF)
    kept_ref[...] = pile_ref[pl.ds(pl.multiple_of(core * half, half), half), :]


def pile_core_kernel(kept_ref, got_ref, own_ref, *piece_refs):
    size = own_ref.shape[0]
    here = 2 * lax.axis_index("y") + lax.axis_index("x")
    for k in range(4):
        at = pl.ds(pl.multiple_of(jnp.bitwise_xor(here, k) * size, size), size)
        value = kept_ref[at, :] + got_ref[at, :].astype(F32)
        if k == 0:
            own_ref[...] = value
        else:
            piece_refs[k - 1][...] = value.astype(BF)


def pile_sum_kernel(own_ref, *refs):
    refs[3][...] = sum_four(own_ref[...].astype(F32), refs[:3], own_ref.shape[0]).astype(refs[3].dtype)


def pile_place_kernel(half_ref, other_ref, out_ref):
    unused, size, unused = half_ref.shape
    here = 2 * lax.axis_index("y") + lax.axis_index("x")
    core = lax.axis_index("c")
    for c, ref in ((0, half_ref), (1, other_ref)):
        for k in range(4):
            at = (jnp.bitwise_xor(core, c) * 4 + jnp.bitwise_xor(here, k)) * size
            out_ref[pl.ds(pl.multiple_of(at, size), size), :] = ref[k].astype(F32)


def sum_pile(away, kept):
    size = away.shape[0] // 4
    width = away.shape[1]
    got = swap(away, 1)
    own, *pieces = run(
        pile_core_kernel, [shape((size, width))] + [shape((size, width), BF)] * 3, [kept, got]
    )
    got = [swap(pieces[k - 1], 2 * k) for k in range(1, 4)]
    if short_line():
        (shard,) = run(pile_sum_kernel, [shape((size, width), BF)], [own, *got])
        got = [pass_line(shard, k) for k in range(1, 4)]
        (shard,) = run(pile_sum_kernel, [shape((size, width), BF)], [shard, *got])
    else:
        (shard,) = run(pile_sum_kernel, [shape((size, width))], [own, *got])
        shard = lax.psum(shard, "z").astype(BF)
    half = jnp.stack([shard] + [swap(shard, 2 * k) for k in range(1, 4)])
    return run(pile_place_kernel, [shape((8 * size, width))], [half, swap(half, 1)])[0]


def center_kernel(near_ref, far_ref, half_ref, other_ref, out_ref):
    count, rows, width = half_ref.shape
    total = dot(near_ref[...], half_ref[...].reshape(count * rows, width))
    total = total + dot(far_ref[...], other_ref[...].reshape(count * rows, width))
    centre_into(out_ref, total)


def per_device(
    features,
    adjacency,
    tile_mask,
    labels,
    train_mask,
    w_first,
    w_second,
    w_head,
    norm_params,
    head_bias,
    m_first,
    m_second,
    m_head,
    m_norms,
    m_bias,
    v_first,
    v_second,
    v_head,
    v_norms,
    v_bias,
):
    rows, node_total = adjacency.shape
    inputs, hidden = w_first.shape
    classes = w_head.shape[1]
    half = node_total // 2
    tall = rows + EXTRA
    second_low = w_second.astype(BF)
    head_low = jnp.pad(w_head, ((0, 0), (0, LANES - classes))).astype(BF)
    bias_row = jnp.pad(head_bias, (0, LANES - classes))[None]
    norm_rows = jnp.pad(norm_params, ((0, 4), (0, 0)))
    inputs_tall = -(-inputs // EXTRA) * EXTRA
    features_turned = jnp.pad(features.T, ((0, inputs_tall - inputs), (0, 0)))
    work = 2 * rows * node_total * hidden

    near, far = run(
        arrange_kernel, [shape((rows, half), BF)] * 2, [tile_mask, adjacency], scalars=1
    )

    projected = dot(features, w_first.astype(BF)).astype(BF)
    (summed_one,) = run(
        center_kernel, [shape((tall, hidden), BF)], [near, far, *gather_all(projected)], flops=work
    )
    around = gather_all(summed_one)
    summed_two, stats_one = run(
        functools.partial(layer_kernel, node_total, 0),
        [shape((tall, hidden), BF), shape((8, hidden))],
        [near, far, second_low, norm_rows, *around],
        flops=3 * work,
    )
    (slopes_one,) = run(
        functools.partial(slopes_kernel, 0),
        [shape((rows, 2 * hidden))],
        [near, far, norm_rows, *around, stats_one],
        flops=3 * work,
    )
    send, turned, parts, stats_two = run(
        functools.partial(head_kernel, node_total, classes),
        [
            shape((HEAD_ROWS + EXTRA, half), BF),
            shape((HEAD_ROWS, rows), BF),
            shape((EXTRA, LANES)),
            shape((8, hidden)),
        ],
        [
            near,
            far,
            head_low,
            norm_rows,
            bias_row,
            labels[:, None],
            train_mask[:, None],
            *gather_all(summed_two),
        ],
        scratch=[pltpu.VMEM((rows, LANES + 2 * hidden), F32), pltpu.VMEM((8, LANES), F32)],
        flops=4 * work,
    )

    own, got, sums = spread_back(turned, send, near, parts)
    send, turned, parts, head_grad, sums_two = run(
        functools.partial(second_kernel, node_total, len(got)),
        [
            shape((hidden + EXTRA, half), BF),
            shape((hidden, rows), BF),
            shape((EXTRA, LANES)),
            shape((HEAD_ROWS, hidden)),
            shape((8, LANES)),
        ],
        [own, *got, *sums, far, head_low, second_low, norm_rows, summed_two, stats_two, slopes_one],
        scratch=[pltpu.VMEM((8, LANES), F32)],
        flops=work // 2,
    )
    own, got, sums = spread_back(turned, send, near, parts)
    send, turned, second_grad, sums_one = run(
        functools.partial(first_kernel, node_total, len(got)),
        [
            shape((hidden, half), BF),
            shape((hidden, rows), BF),
            shape((hidden, hidden)),
            shape((8, LANES)),
        ],
        [own, *got, *sums, far, second_low, norm_rows, summed_one, stats_one],
        flops=work // 2,
    )
    own, got, sums = spread_back(turned, send, near, None)
    length = inputs_tall + hidden + HEAD_ROWS
    size = -(-length // (8 * EXTRA)) * EXTRA
    away, kept = run(
        functools.partial(pile_kernel, len(got)),
        [shape((4 * size, hidden), BF), shape((4 * size, hidden))],
        [own, *got, features_turned, second_grad, head_grad],
        scratch=[pltpu.VMEM((8 * size, hidden), F32)],
    )
    pile = sum_pile(away, kept)
    first_grad = pile[:inputs]
    second_grad = pile[inputs_tall : inputs_tall + hidden]
    head_grad = pile[inputs_tall + hidden : inputs_tall + hidden + classes].T

    def pair(sums):
        return sums[2:4].reshape(1, hidden), sums[0:2].reshape(1, hidden)

    norm_grad = jnp.concatenate([*pair(sums_one), *pair(sums_two)])
    bias_grad = sums_two[4, :classes]
    params = (w_first, w_second, w_head, norm_params, head_bias)
    grads = (first_grad, second_grad, head_grad, norm_grad, bias_grad)
    firsts = (m_first, m_second, m_head, m_norms, m_bias)
    seconds = (v_first, v_second, v_head, v_norms, v_bias)
    rates = (RATE_MATRIX, RATE_MATRIX, RATE_MATRIX, RATE_SMALL, RATE_SMALL)
    updated = [adamw(params[i], grads[i], firsts[i], seconds[i], rates[i]) for i in range(5)]
    return (
        sums_two[5, 0],
        sums_two[5, 1],
        *(updated[i][0] for i in range(5)),
        *(updated[i][1] for i in range(5)),
        *(updated[i][2] for i in range(5)),
    )


def solution(mesh):
    wide_mesh = Mesh(mesh.devices.reshape(-1, 2, 2, 2), EVERY)
    split = (P(EVERY, None),) * 3 + (P(EVERY),) * 2
    return jax.shard_map(
        per_device,
        mesh=wide_mesh,
        in_specs=split + (P(),) * 15,
        out_specs=(P(),) * 17,
        check_vma=False,
    )
```

```python
import functools
import math

import jax
import jax.numpy as jnp
from jax import lax
from jax.experimental import pallas as pl
from jax.experimental.pallas import tpu as pltpu
from jax.sharding import Mesh
from jax.sharding import PartitionSpec as P

TILE = 128
STEP = 10
EPS_NORM = 1e-05
EPS_ADAM = 1e-08
BETA_ONE = 0.9
BETA_TWO = 0.999
DECAY = 0.01
RATE_MATRIX = 0.03
RATE_SMALL = 0.3

BF = jnp.bfloat16
F32 = jnp.float32
PLANE = ("y", "x", "c")
EVERY = ("z", "y", "x", "c")
LANES = 128
HEAD_ROWS = 48
EXTRA = 16
ROOT = math.sqrt(2.0 / math.pi)
BEND = 0.044715


def adamw(weight, gradient, first, second, rate):
    first_new = BETA_ONE * first + (1.0 - BETA_ONE) * gradient
    second_new = BETA_TWO * second + (1.0 - BETA_TWO) * gradient * gradient
    scaled = (
        first_new
        / (1.0 - BETA_ONE**STEP)
        / (jnp.sqrt(second_new / (1.0 - BETA_TWO**STEP)) + EPS_ADAM)
    )
    return (weight - rate * (scaled + DECAY * weight), first_new, second_new)


def dot(left, right):
    return jnp.dot(left, right, preferred_element_type=F32)


def dot_turned(left, right):
    return lax.dot_general(left, right, (((1,), (1,)), ((), ())), preferred_element_type=F32)


def shape(dims, kind=F32):
    return jax.ShapeDtypeStruct(dims, kind)


def run(body, outs, ins, scratch=(), flops=0, scalars=0):
    held = sum(math.prod(a.shape[:-1]) * max(a.shape[-1], LANES) * a.dtype.itemsize for a in (*ins, *outs))
    limit = min(60 << 20, 2 * held + (8 << 20))
    return pl.pallas_call(
        body,
        out_shape=tuple(outs),
        in_specs=[pl.BlockSpec(memory_space=pltpu.SMEM)] * scalars
        + [pl.BlockSpec(memory_space=pltpu.VMEM)] * (len(ins) - scalars),
        out_specs=tuple(pl.BlockSpec(memory_space=pltpu.VMEM) for unused in outs),
        scratch_shapes=list(scratch),
        compiler_params=pltpu.CompilerParams(vmem_limit_bytes=limit),
        cost_estimate=pl.CostEstimate(flops=flops, bytes_accessed=held, transcendentals=0),
    )(*ins)


def swap(block, mask):
    return lax.ppermute(block, PLANE, [(i, i ^ mask) for i in range(8)])


def pass_line(block, mask):
    return lax.ppermute(block, "z", [(i, i ^ mask) for i in range(4)])


def short_line():
    return lax.axis_size("z") == 4


def after(block, *others):
    return lax.optimization_barrier((block, *others))[0]


def gather_all(block, beside=()):
    if short_line():
        line = jnp.stack([block] + [pass_line(block, k) for k in range(1, 4)])
    else:
        line = lax.all_gather(block, "z", axis=0)
    passed = [pass_line(after(part, line), mask) for part, mask in beside]
    lines = [line] + [swap(line, 2 * k) for k in range(1, 4)]
    if passed:
        held = lax.optimization_barrier((*lines, *passed))
        lines, passed = list(held[:4]), list(held[4:])
    return lines + [swap(line, 1) for line in lines], passed


def arrange_kernel(mask_ref, values_ref, near_ref, far_ref, *level_refs):
    half = near_ref.shape[1] // TILE
    lines = half // 4
    here = 4 * lax.axis_index("y") + 2 * lax.axis_index("x") + lax.axis_index("c")
    level = lax.axis_index("z") if short_line() else 0

    for core, out_ref in ((0, near_ref), (1, far_ref)):
        for place in range(4):

            def one(step, carry, core=core, place=place, out_ref=out_ref):
                source = jnp.bitwise_xor(step, level) * 8 + jnp.bitwise_xor(place * 2 + core, here)
                keep = mask_ref[0, source].astype(F32).astype(BF)
                block = values_ref[:, pl.ds(pl.multiple_of(source * TILE, TILE), TILE)] * keep
                at = pl.multiple_of((place * lines + step) * TILE, TILE)
                out_ref[:, pl.ds(at, TILE)] = block
                cols = slice((core * 4 + place) * TILE, (core * 4 + place + 1) * TILE)
                if len(level_refs) == 1:
                    level_refs[0][step, :, cols] = block
                else:
                    level_refs[step][:, cols] = block
                return carry

            if len(level_refs) == 1:
                lax.fori_loop(0, lines, one, 0)
            else:
                for step in range(lines):
                    one(step, 0)


def centre_into(out_ref, summed):
    rows = summed.shape[0]
    centre = (jnp.sum(summed, axis=0, keepdims=True) / rows).astype(BF).astype(F32)
    out_ref[:rows, :] = (summed - centre).astype(BF)
    out_ref[rows:, :] = jnp.broadcast_to(centre, (EXTRA, summed.shape[1])).astype(BF)


def moments(refs, node_total):
    count, tall, width = refs[0].shape
    rows = tall - EXTRA
    pivot = refs[0][0, rows:, :].astype(F32)[:1]
    zero = jnp.zeros((8, width), F32)
    sums = (zero, zero)
    for ref in refs:

        def one(i, carry, ref=ref):
            total, square = carry
            value = ref[i, :rows, :].astype(F32).reshape(rows // 8, 8, width)
            part = jnp.sum(value, axis=0)
            away = ref[i, rows:, :].astype(F32)[:1] - pivot
            each = away * (rows // 8)
            return (
                total + part + each,
                square + jnp.sum(value * value, axis=0) + away * (2.0 * part + each),
            )

        sums = lax.fori_loop(0, count, one, sums, unroll=4)
    shift = jnp.sum(sums[0], axis=0, keepdims=True) / node_total
    variance = jnp.sum(sums[1], axis=0, keepdims=True) / node_total - shift * shift
    return pivot + shift, lax.rsqrt(jnp.maximum(variance, 0.0) + EPS_NORM)


def gelu_half(value):
    square = value * value
    bend = jnp.tanh(value * (ROOT + (ROOT * BEND) * square))
    return 0.5 + 0.5 * bend, bend, square


def gelu_slope(value, half, bend, square):
    return half + (0.5 * value) * (1.0 - bend * bend) * (ROOT + (3 * ROOT * BEND) * square)


def blocks_of(ref, i, pair, rows):
    parts = [
        (ref[i * pair + j, :rows, :].astype(F32), ref[i * pair + j, rows:, :].astype(F32)[:1])
        for j in range(pair)
    ]
    return parts


def with_columns(refs, near_ref, far_ref, rows, pair, act, total):
    count = refs[0].shape[0]
    for n, ref in enumerate(refs):
        adjacent_ref = far_ref if n >= 4 else near_ref

        def one(i, total, ref=ref, adjacent_ref=adjacent_ref, at=n % 4 * count * rows):
            start = pl.multiple_of(at + i * (pair * rows), pair * rows)
            return act(
                blocks_of(ref, i, pair, rows), adjacent_ref[:, pl.ds(start, pair * rows)], total
            )

        total = lax.fori_loop(0, count // pair, one, total, unroll=2)
    return total


def split_sums(total):
    high = total.astype(BF).astype(F32)
    low = (total - high).astype(BF).astype(F32)
    return jnp.concatenate([high, low])


def joined(parts):
    parts = parts.astype(F32)
    return parts[: EXTRA // 2] + parts[EXTRA // 2 :]


def put_sums(out_ref, width, parts):
    out_ref[width:, :LANES] = parts.astype(BF)
    if out_ref.shape[1] > LANES:
        out_ref[width:, LANES:] = jnp.zeros((EXTRA, out_ref.shape[1] - LANES), BF)


def pack_into(out_ref, turned, parts):
    width = turned.shape[0]
    out_ref[:width, :] = turned.astype(BF)
    if parts is not None:
        put_sums(out_ref, width, parts)


def add_up(values):
    values = list(values)
    while len(values) > 1:
        values = [values[i] + values[i + 1] for i in range(0, len(values), 2)]
    return values[0]


def cross(turned_refs, level_refs, start, stop, width, out):
    if len(level_refs) == 1:
        count = level_refs[0].shape[0]
        turned = [turned_refs[0].at[i] for i in range(count)]
        levels = [level_refs[0].at[i] for i in range(count)]
    else:
        turned, levels = turned_refs, level_refs
    total = None
    for i in range(0, len(levels), 2):
        left = jnp.concatenate([turned[i][:width, :], turned[i + 1][:width, :]], axis=1)
        right = jnp.concatenate([levels[i][:, start:stop], levels[i + 1][:, start:stop]])
        part = dot(left, right)
        total = part if total is None else total + part
    out(total)


def cross_kernel(width, count, *refs):
    turned_refs, level_refs, (send_ref,) = refs[:count], refs[count : 2 * count], refs[2 * count :]
    half = send_ref.shape[1]

    def out(value):
        send_ref[:width, :] = value.astype(BF)

    cross(turned_refs, level_refs, half, 2 * half, width, out)
    if send_ref.shape[0] > width:
        if count == 1:
            parts = [joined(turned_refs[0][i, width:, :]) for i in range(turned_refs[0].shape[0])]
        else:
            parts = [joined(ref[width:, :]) for ref in turned_refs]
        put_sums(send_ref, width, split_sums(add_up(parts)))


def keep_kernel(width, count, *refs):
    turned_refs, level_refs, (out_ref,) = refs[:count], refs[count : 2 * count], refs[2 * count :]

    def out(value):
        out_ref[...] = value

    cross(turned_refs, level_refs, 0, out_ref.shape[1], width, out)


def fold_kernel(kept_ref, send_ref, got_ref, own_ref, *piece_refs):
    width = kept_ref.shape[0]
    for k in range(4):
        cols = slice(k * LANES, (k + 1) * LANES)
        value = kept_ref[:, cols] + got_ref[:width, cols].astype(F32)
        if k == 0:
            own_ref[:width, :] = value
        else:
            piece_refs[k - 1][:width, :] = value.astype(BF)
    if own_ref.shape[0] > width:
        parts = split_sums(joined(send_ref[width:, :LANES]) + joined(got_ref[width:, :LANES]))
        own_ref[width:, :] = parts
        for piece_ref in piece_refs:
            put_sums(piece_ref, width, parts)


def spread_back(packed, levels, width):
    tall = packed.shape[0]
    if short_line():
        turned = [packed] + [pass_line(packed, k) for k in range(1, 4)]
    else:
        turned = [lax.all_gather(packed, "z", axis=0)]
    count = len(levels)
    half = levels[0].shape[-1] // 2
    work = 8 * width * LANES * half
    (send,) = run(
        functools.partial(cross_kernel, width, count),
        [shape((tall, half), BF)],
        [*turned, *levels],
        flops=work,
    )
    got = swap(send, 1)
    (kept,) = run(
        functools.partial(keep_kernel, width, count),
        [shape((width, half))],
        [*turned, *levels],
        flops=work,
    )
    own, *pieces = run(
        fold_kernel, [shape((tall, LANES))] + [shape((tall, LANES), BF)] * 3, [kept, send, got]
    )
    return [own] + [swap(pieces[k - 1], 2 * k) for k in range(1, 4)]


def line_total(refs, width):
    total = add_up(ref[:width, :].astype(F32) for ref in refs)
    if refs[0].shape[0] == width:
        return total, None
    return total, add_up(joined(ref[width:, :]) for ref in refs)


def wide(sums, row):
    return jnp.concatenate([sums[row : row + 1], sums[row + 1 : row + 2]], axis=1)


def put_wide(ref, row, value):
    ref[row : row + 1, :] = value[:, :LANES]
    ref[row + 1 : row + 2, :] = value[:, LANES:]


def layer_kernel(node_total, layer, near_ref, far_ref, weight_ref, norm_ref, *refs):
    refs, (out_ref, stats_ref) = refs[:8], refs[8:]
    count, tall, width = refs[0].shape
    rows = tall - EXTRA
    mean_value, inverse = moments(refs, node_total)
    stats_ref[0:1, :] = mean_value
    stats_ref[1:2, :] = inverse
    scale = norm_ref[2 * layer : 2 * layer + 1, :] * inverse
    start = norm_ref[2 * layer + 1 : 2 * layer + 2, :] - mean_value * scale
    low = weight_ref[...].astype(BF)

    def act(blocks, adjacent, total):
        hidden = []
        for value, centre in blocks:
            value = value * scale + (start + centre * scale)
            hidden.append((value * gelu_half(value)[0]).astype(BF))
        projected = dot(jnp.concatenate(hidden), low).astype(BF)
        return total + dot(adjacent, projected)

    total = jnp.zeros((rows, low.shape[1]), F32)
    centre_into(out_ref, with_columns(refs, near_ref, far_ref, rows, 2, act, total))


def slopes_kernel(layer, near_ref, far_ref, norm_ref, stats_ref, *refs):
    refs, out_ref = refs[:8], refs[8]
    count, tall, width = refs[0].shape
    rows = tall - EXTRA
    mean_value, inverse = stats_ref[0:1, :], stats_ref[1:2, :]
    gain = norm_ref[2 * layer : 2 * layer + 1, :]
    offset = norm_ref[2 * layer + 1 : 2 * layer + 2, :]
    out_ref[...] = jnp.zeros(out_ref.shape, F32)

    def act(blocks, adjacent, carry):
        slopes = []
        for value, centre in blocks:
            normed = value * inverse + (centre - mean_value) * inverse
            value = gain * normed + offset
            slope = gelu_slope(value, *gelu_half(value))
            slopes.append(jnp.concatenate([slope.astype(BF), (slope * normed).astype(BF)], axis=1))
        out_ref[...] += dot(adjacent, jnp.concatenate(slopes))
        return carry

    with_columns(refs, near_ref, far_ref, rows, 2, act, 0)


def head_low_of(weight_ref, tall_ref):
    tall_ref[...] = jnp.zeros(tall_ref.shape, F32)
    tall_ref[: weight_ref.shape[0], :] = weight_ref[...]
    return tall_ref[...].astype(BF)


def head_kernel(
    node_total, near_ref, far_ref, weight_ref, norm_ref, bias_ref, label_ref, mask_ref, *refs
):
    refs, (packed_ref, stats_ref, total_ref, sums_ref, tall_ref) = refs[:8], refs[8:]
    count, tall, width = refs[0].shape
    rows = tall - EXTRA
    classes = weight_ref.shape[0]
    mean_value, inverse = moments(refs, node_total)
    stats_ref[0:1, :] = mean_value
    stats_ref[1:2, :] = inverse
    gain, offset = norm_ref[2:3, :], norm_ref[3:4, :]
    low = head_low_of(weight_ref, tall_ref)
    total_ref[...] = jnp.zeros(total_ref.shape, F32)

    def act(blocks, adjacent, carry):
        hidden, slopes = [], []
        for value, centre in blocks:
            normed = value * inverse + (centre - mean_value) * inverse
            value = gain * normed + offset
            half, bend, square = gelu_half(value)
            slope = gelu_slope(value, half, bend, square)
            hidden.append((value * half).astype(BF))
            slopes.append(jnp.concatenate([slope.astype(BF), (slope * normed).astype(BF)], axis=1))
        headed = dot_turned(jnp.concatenate(hidden), low).astype(BF)
        both = jnp.concatenate([headed, jnp.concatenate(slopes)], axis=1)
        total_ref[...] += dot(adjacent, both)
        return carry

    with_columns(refs, near_ref, far_ref, rows, 2, act, 0)

    lane = lax.broadcasted_iota(jnp.int32, (rows, LANES), 1)
    sums_ref[...] = jnp.zeros(sums_ref.shape, F32)
    sums_ref[:1, :classes] = bias_ref[...]
    logits = jnp.where(lane < classes, total_ref[:, :LANES] + sums_ref[:1, :], -1e30)
    logits = logits - jnp.max(logits, axis=1, keepdims=True)
    raised = jnp.exp(logits)
    whole = jnp.sum(raised, axis=1, keepdims=True)
    label = jnp.broadcast_to(label_ref[...].astype(F32), (LANES, rows)).T
    onehot = jnp.where(lane.astype(F32) == label, 1.0, 0.0)
    weight = jnp.broadcast_to(mask_ref[...].astype(F32), (LANES, rows)).T
    losses = jnp.log(whole) - jnp.sum(onehot * logits, axis=1, keepdims=True)
    d_logits = (raised / whole - onehot) * weight
    d_low = d_logits.astype(BF)
    d_wide = dot(d_low, low)
    put_wide(sums_ref, 0, jnp.sum(d_wide * total_ref[:, LANES : LANES + width], axis=0, keepdims=True))
    put_wide(sums_ref, 2, jnp.sum(d_wide * total_ref[:, LANES + width :], axis=0, keepdims=True))
    sums_ref[4:5, :] = jnp.sum(d_logits, axis=0, keepdims=True)
    sums_ref[5:6, :] = jnp.sum(
        jnp.where(lane == 0, losses * weight, weight), axis=0, keepdims=True
    )
    pack_into(packed_ref, d_logits.T[:HEAD_ROWS], split_sums(sums_ref[...]))


def backward_norm(d_hidden, own_ref, stats_ref, norm_ref, layer, shift_grad, gain_grad, node_total):
    rows = own_ref.shape[0] - EXTRA
    mean_value, inverse = stats_ref[0:1, :], stats_ref[1:2, :]
    gain = norm_ref[2 * layer : 2 * layer + 1, :]
    centre = own_ref[rows:, :].astype(F32)[:1]
    normed = own_ref[:rows, :].astype(F32) * inverse + (centre - mean_value) * inverse
    value = gain * normed + norm_ref[2 * layer + 1 : 2 * layer + 2, :]
    half, bend, square = gelu_half(value)
    d_pre = d_hidden * gelu_slope(value, half, bend, square)
    d_summed = (gain * inverse) * (d_pre - (shift_grad + normed * gain_grad) / node_total)
    return d_summed, value * half


def second_kernel(
    node_total,
    head_ref,
    weight_ref,
    norm_ref,
    summed_ref,
    stats_ref,
    slopes_ref,
    *refs,
):
    refs, (packed_ref, grad_ref, out_ref, sums_ref, tall_ref) = refs[:4], refs[4:]
    headed, sums = line_total(refs, HEAD_ROWS)
    rows = headed.shape[1]
    each = 1.0 / sums[5:6, 1:2]
    headed = headed * each
    put_row = lax.broadcasted_iota(jnp.int32, sums.shape, 0)
    out_ref[...] = jnp.where(put_row == 5, sums, sums * each)
    turned_back = jnp.concatenate([headed, jnp.zeros((LANES - HEAD_ROWS, rows), F32)]).T
    d_hidden = dot(turned_back.astype(BF), head_low_of(head_ref, tall_ref))
    d_summed, hidden = backward_norm(
        d_hidden, summed_ref, stats_ref, norm_ref, 1, wide(sums, 0) * each, wide(sums, 2) * each, node_total
    )
    grad_ref[...] = dot(headed.astype(BF), hidden.astype(BF))
    d_wide = dot_turned(d_summed.astype(BF), weight_ref[...].astype(BF))
    width = d_wide.shape[1]
    put_wide(sums_ref, 0, jnp.sum(d_wide * slopes_ref[:, :width], axis=0, keepdims=True))
    put_wide(sums_ref, 2, jnp.sum(d_wide * slopes_ref[:, width:], axis=0, keepdims=True))
    sums_ref[4:8, :] = jnp.zeros((4, LANES), F32)
    pack_into(packed_ref, d_summed.T, split_sums(sums_ref[...]))


def first_kernel(node_total, weight_ref, norm_ref, summed_ref, stats_ref, *refs):
    refs, (packed_ref, grad_ref, out_ref) = refs[:4], refs[4:]
    d_projected, sums = line_total(refs, weight_ref.shape[1])
    out_ref[...] = sums
    d_projected = d_projected.T.astype(BF)
    d_hidden = dot_turned(d_projected, weight_ref[...].astype(BF))
    d_summed, hidden = backward_norm(
        d_hidden, summed_ref, stats_ref, norm_ref, 0, wide(sums, 0), wide(sums, 2), node_total
    )
    pack_into(packed_ref, d_summed.T, None)
    grad_ref[...] = dot(hidden.T.astype(BF), d_projected)


def pile_kernel(inputs_tall, inputs_ref, second_ref, head_ref, *refs):
    refs, (away_ref, kept_ref, pile_ref) = refs[:4], refs[4:]
    d_projected = line_total(refs, second_ref.shape[0])[0].T.astype(BF)
    pile_ref[...] = jnp.zeros(pile_ref.shape, F32)
    pile_ref[: inputs_ref.shape[0], :] = dot(inputs_ref[...], d_projected)
    at = inputs_tall
    pile_ref[at : at + second_ref.shape[0], :] = second_ref[...]
    at += second_ref.shape[0]
    pile_ref[at : at + HEAD_ROWS, :] = head_ref[...]
    half = away_ref.shape[0]
    core = lax.axis_index("c")
    away_ref[...] = pile_ref[pl.ds(pl.multiple_of((1 - core) * half, half), half), :].astype(BF)
    kept_ref[...] = pile_ref[pl.ds(pl.multiple_of(core * half, half), half), :]


def pile_core_kernel(kept_ref, got_ref, own_ref, *piece_refs):
    size = own_ref.shape[0]
    here = 2 * lax.axis_index("y") + lax.axis_index("x")
    for k in range(4):
        at = pl.ds(pl.multiple_of(jnp.bitwise_xor(here, k) * size, size), size)
        value = kept_ref[at, :] + got_ref[at, :].astype(F32)
        if k == 0:
            own_ref[...] = value
        else:
            piece_refs[k - 1][...] = value.astype(BF)


def pile_sum_kernel(own_ref, *refs):
    parts = [own_ref, *refs[:3]]
    refs[3][...] = add_up(ref[...].astype(F32) for ref in parts).astype(refs[3].dtype)


def update_kernel(inputs_tall, *refs):
    pieces, refs = refs[:8], refs[8:]
    inputs, outs, pile_ref = refs[:9], refs[9:18], refs[18]
    size, width = pieces[0].shape
    here = 2 * lax.axis_index("y") + lax.axis_index("x")
    core = lax.axis_index("c")
    for n, ref in enumerate(pieces):
        at = (jnp.bitwise_xor(core, n // 4) * 4 + jnp.bitwise_xor(here, n % 4)) * size
        pile_ref[pl.ds(pl.multiple_of(at, size), size), :] = ref[...].astype(F32)
    tall = inputs[0].shape[0]
    grads = (
        pile_ref[:tall, :],
        pile_ref[inputs_tall : inputs_tall + width, :],
        pile_ref[inputs_tall + width : inputs_tall + width + inputs[6].shape[0], :],
    )
    for n in range(3):
        weight, first, second = (ref[...] for ref in inputs[3 * n : 3 * n + 3])
        results = adamw(weight, grads[n], first, second, RATE_MATRIX)
        for ref, value in zip(outs[3 * n : 3 * n + 3], results, strict=True):
            ref[...] = value


def sum_pile(away, kept):
    size = away.shape[0] // 4
    width = away.shape[1]
    got = swap(away, 1)
    own, *pieces = run(
        pile_core_kernel, [shape((size, width))] + [shape((size, width), BF)] * 3, [kept, got]
    )
    got = [swap(pieces[k - 1], 2 * k) for k in range(1, 4)]
    if short_line():
        (shard,) = run(pile_sum_kernel, [shape((size, width), BF)], [own, *got])
        got = [pass_line(shard, k) for k in range(1, 4)]
        (shard,) = run(pile_sum_kernel, [shape((size, width), BF)], [shard, *got])
    else:
        (shard,) = run(pile_sum_kernel, [shape((size, width))], [own, *got])
        shard = lax.psum(shard, "z").astype(BF)
    pieces = [shard] + [swap(shard, 2 * k) for k in range(1, 4)]
    return pieces + [swap(piece, 1) for piece in pieces]


def first_sum_kernel(near_ref, far_ref, *refs):
    refs, out_ref = refs[:8], refs[8]
    count, rows, width = refs[0].shape
    total = jnp.zeros((rows, width), F32)
    for n, ref in enumerate(refs):
        adjacent_ref = far_ref if n >= 4 else near_ref
        at = n % 4 * count * rows
        total = total + dot(
            adjacent_ref[:, at : at + count * rows], ref[...].reshape(count * rows, width)
        )
    centre_into(out_ref, total)


def per_device(
    features,
    adjacency,
    tile_mask,
    labels,
    train_mask,
    w_first,
    w_second,
    w_head,
    norm_params,
    head_bias,
    m_first,
    m_second,
    m_head,
    m_norms,
    m_bias,
    v_first,
    v_second,
    v_head,
    v_norms,
    v_bias,
):
    rows, node_total = adjacency.shape
    inputs, hidden = w_first.shape
    classes = w_head.shape[1]
    half = node_total // 2
    length = lax.axis_size("z")
    tall = rows + EXTRA
    inputs_tall = -(-inputs // EXTRA) * EXTRA
    head_turned = w_head.T
    work = 2 * rows * node_total * hidden

    if short_line():
        level_shapes = [shape((rows, 8 * rows), BF)] * 4
    else:
        level_shapes = [shape((length, rows, 8 * rows), BF)]
    near, far, *levels = run(
        arrange_kernel,
        [shape((rows, half), BF)] * 2 + level_shapes,
        [tile_mask, adjacency],
        scalars=1,
    )

    projected = dot(features, w_first.astype(BF)).astype(BF)
    if short_line():
        around, passed = gather_all(projected, [(levels[1], 1), (levels[2], 2)])
        levels[1:3] = passed
    else:
        around, passed = gather_all(projected)
        levels = [lax.all_to_all(levels[0], "z", 0, 0)]
    (summed_one,) = run(
        first_sum_kernel, [shape((tall, hidden), BF)], [near, far, *around], flops=work
    )
    if short_line():
        around, passed = gather_all(summed_one, [(levels[3], 3)])
        levels[3:] = passed
    else:
        around, passed = gather_all(summed_one)
    summed_two, stats_one = run(
        functools.partial(layer_kernel, node_total, 0),
        [shape((tall, hidden), BF), shape((8, hidden))],
        [near, far, w_second, norm_params, *around],
        flops=3 * work,
    )
    (slopes_one,) = run(
        functools.partial(slopes_kernel, 0),
        [shape((rows, 2 * hidden))],
        [near, far, norm_params, stats_one, *around],
        flops=3 * work,
    )
    packed, stats_two = run(
        functools.partial(head_kernel, node_total),
        [shape((HEAD_ROWS + EXTRA, rows), BF), shape((8, hidden))],
        [
            near,
            far,
            head_turned,
            norm_params,
            head_bias[None],
            labels[None],
            train_mask[None],
            *gather_all(summed_two)[0],
        ],
        scratch=[
            pltpu.VMEM((rows, LANES + 2 * hidden), F32),
            pltpu.VMEM((8, LANES), F32),
            pltpu.VMEM((LANES, hidden), F32),
        ],
        flops=4 * work,
    )

    packed, head_grad, sums_two = run(
        functools.partial(second_kernel, node_total),
        [shape((hidden + EXTRA, rows), BF), shape((HEAD_ROWS, hidden)), shape((8, LANES))],
        [
            head_turned,
            w_second,
            norm_params,
            summed_two,
            stats_two,
            slopes_one,
            *spread_back(packed, levels, HEAD_ROWS),
        ],
        scratch=[pltpu.VMEM((8, LANES), F32), pltpu.VMEM((LANES, hidden), F32)],
        flops=work // 4,
    )
    packed, second_grad, sums_one = run(
        functools.partial(first_kernel, node_total),
        [shape((hidden, rows), BF), shape((hidden, hidden)), shape((8, LANES))],
        [w_second, norm_params, summed_one, stats_one, *spread_back(packed, levels, hidden)],
        flops=work // 4,
    )
    size = -(-(inputs_tall + hidden + HEAD_ROWS) // (8 * EXTRA)) * EXTRA
    away, kept = run(
        functools.partial(pile_kernel, inputs_tall),
        [shape((4 * size, hidden), BF), shape((4 * size, hidden))],
        [features.T, second_grad, head_grad, *spread_back(packed, levels, hidden)],
        scratch=[pltpu.VMEM((8 * size, hidden), F32)],
    )
    matrices = (
        *(w_first, m_first, v_first, w_second, m_second, v_second),
        *(head_turned, m_head.T, v_head.T),
    )
    updated = run(
        functools.partial(update_kernel, inputs_tall),
        [shape(block.shape) for block in matrices],
        [*sum_pile(away, kept), *matrices],
        scratch=[pltpu.VMEM((8 * size, hidden), F32)],
    )
    updated = [*updated[:6], *(block.T for block in updated[6:])]

    def pair(sums):
        return sums[2:4].reshape(1, hidden), sums[0:2].reshape(1, hidden)

    norm_grad = jnp.concatenate([*pair(sums_one), *pair(sums_two)])
    norms = adamw(norm_params, norm_grad, m_norms, v_norms, RATE_SMALL)
    bias = adamw(head_bias, sums_two[4, :classes], m_bias, v_bias, RATE_SMALL)
    loss_sum, train_count = sums_two[5, 0], sums_two[5, 1]
    return (
        loss_sum,
        train_count,
        *(
            part
            for n in range(3)
            for part in (updated[n], updated[3 + n], updated[6 + n], norms[n], bias[n])
        ),
    )


def solution(mesh):
    wide_mesh = Mesh(mesh.devices.reshape(-1, 2, 2, 2), EVERY)
    split = (P(EVERY, None),) * 3 + (P(EVERY),) * 2
    return jax.shard_map(
        per_device,
        mesh=wide_mesh,
        in_specs=split + (P(),) * 15,
        out_specs=(P(),) * 17,
        check_vma=False,
    )
```

```python
import functools
import math

import jax
import jax.numpy as jnp
from jax import lax
from jax.experimental import pallas as pl
from jax.experimental.pallas import tpu as pltpu
from jax.sharding import Mesh
from jax.sharding import PartitionSpec as P

TILE = 128
STEP = 10
EPS_NORM = 1e-05
EPS_ADAM = 1e-08
BETA_ONE = 0.9
BETA_TWO = 0.999
DECAY = 0.01
RATE_MATRIX = 0.03
RATE_SMALL = 0.3

BF = jnp.bfloat16
F32 = jnp.float32
PLANE = ("y", "x", "c")
EVERY = ("z", "y", "x", "c")
LANES = 128
HEAD_ROWS = 48
EXTRA = 16
ROOT = math.sqrt(2.0 / math.pi)
BEND = 0.044715


def adamw(weight, gradient, first, second, rate):
    first_new = BETA_ONE * first + (1.0 - BETA_ONE) * gradient
    second_new = BETA_TWO * second + (1.0 - BETA_TWO) * gradient * gradient
    scaled = (
        first_new
        / (1.0 - BETA_ONE**STEP)
        / (jnp.sqrt(second_new / (1.0 - BETA_TWO**STEP)) + EPS_ADAM)
    )
    return (weight - rate * (scaled + DECAY * weight), first_new, second_new)


def dot(left, right):
    return jnp.dot(left, right, preferred_element_type=F32)


def dot_turned(left, right):
    return lax.dot_general(left, right, (((1,), (1,)), ((), ())), preferred_element_type=F32)


def shape(dims, kind=F32):
    return jax.ShapeDtypeStruct(dims, kind)


def run(body, outs, ins, scratch=(), flops=0, scalars=0):
    held = sum(math.prod(a.shape[:-1]) * max(a.shape[-1], LANES) * a.dtype.itemsize for a in (*ins, *outs))
    limit = min(60 << 20, 2 * held + (8 << 20))
    return pl.pallas_call(
        body,
        out_shape=tuple(outs),
        in_specs=[pl.BlockSpec(memory_space=pltpu.SMEM)] * scalars
        + [pl.BlockSpec(memory_space=pltpu.VMEM)] * (len(ins) - scalars),
        out_specs=tuple(pl.BlockSpec(memory_space=pltpu.VMEM) for unused in outs),
        scratch_shapes=list(scratch),
        compiler_params=pltpu.CompilerParams(vmem_limit_bytes=limit),
        cost_estimate=pl.CostEstimate(flops=flops, bytes_accessed=held, transcendentals=0),
    )(*ins)


def swap(block, mask):
    return lax.ppermute(block, PLANE, [(i, i ^ mask) for i in range(8)])


def pass_line(block, mask):
    return lax.ppermute(block, "z", [(i, i ^ mask) for i in range(4)])


def short_line():
    return lax.axis_size("z") == 4


def after(block, *others):
    return lax.optimization_barrier((block, *others))[0]


def gather_all(block, beside=(), early=()):
    if short_line():
        line = jnp.stack([block] + [pass_line(block, k) for k in range(1, 4)])
    else:
        line = lax.all_gather(block, "z", axis=0)
    if early:
        line, *early = lax.optimization_barrier((line, *early))
    passed = [pass_line(after(part, line), mask) for part, mask in beside]
    lines = [line] + [swap(line, 2 * k) for k in range(1, 4)]
    if passed:
        lines[3], *passed = lax.optimization_barrier((lines[3], *passed))
    return lines + [swap(line, 1) for line in lines], passed, early


def arrange_kernel(mask_ref, values_ref, near_ref, far_ref, *level_refs):
    half = near_ref.shape[1] // TILE
    lines = half // 4
    here = 4 * lax.axis_index("y") + 2 * lax.axis_index("x") + lax.axis_index("c")
    level = lax.axis_index("z") if short_line() else 0

    for core, out_ref in ((0, near_ref), (1, far_ref)):
        for place in range(4):

            def one(step, carry, core=core, place=place, out_ref=out_ref):
                source = jnp.bitwise_xor(step, level) * 8 + jnp.bitwise_xor(place * 2 + core, here)
                keep = mask_ref[0, source].astype(F32).astype(BF)
                block = values_ref[:, pl.ds(pl.multiple_of(source * TILE, TILE), TILE)] * keep
                at = pl.multiple_of((place * lines + step) * TILE, TILE)
                out_ref[:, pl.ds(at, TILE)] = block
                cols = slice((core * 4 + place) * TILE, (core * 4 + place + 1) * TILE)
                if len(level_refs) == 1:
                    level_refs[0][step, :, cols] = block
                else:
                    level_refs[step][:, cols] = block
                return carry

            if len(level_refs) == 1:
                lax.fori_loop(0, lines, one, 0)
            else:
                for step in range(lines):
                    one(step, 0)


def centre_into(out_ref, summed):
    rows = summed.shape[0]
    centre = (jnp.sum(summed, axis=0, keepdims=True) / rows).astype(BF).astype(F32)
    out_ref[:rows, :] = (summed - centre).astype(BF)
    out_ref[rows:, :] = jnp.broadcast_to(centre, (EXTRA, summed.shape[1])).astype(BF)


def moments(refs, node_total):
    count, tall, width = refs[0].shape
    rows = tall - EXTRA
    pivot = refs[0][0, rows:, :].astype(F32)[:1]
    zero = jnp.zeros((8, width), F32)
    sums = (zero, zero)
    for ref in refs:

        def one(i, carry, ref=ref):
            total, square = carry
            value = ref[i, :rows, :].astype(F32).reshape(rows // 8, 8, width)
            part = jnp.sum(value, axis=0)
            away = ref[i, rows:, :].astype(F32)[:1] - pivot
            each = away * (rows // 8)
            return (
                total + part + each,
                square + jnp.sum(value * value, axis=0) + away * (2.0 * part + each),
            )

        sums = lax.fori_loop(0, count, one, sums, unroll=4)
    shift = jnp.sum(sums[0], axis=0, keepdims=True) / node_total
    variance = jnp.sum(sums[1], axis=0, keepdims=True) / node_total - shift * shift
    return pivot + shift, lax.rsqrt(jnp.maximum(variance, 0.0) + EPS_NORM)


def gelu_half(value):
    square = value * value
    bend = jnp.tanh(value * (ROOT + (ROOT * BEND) * square))
    return 0.5 + 0.5 * bend, bend, square


def gelu_slope(value, half, bend, square):
    return half + (0.5 * value) * (1.0 - bend * bend) * (ROOT + (3 * ROOT * BEND) * square)


def blocks_of(ref, i, pair, rows):
    parts = [
        (ref[i * pair + j, :rows, :].astype(F32), ref[i * pair + j, rows:, :].astype(F32)[:1])
        for j in range(pair)
    ]
    return parts


def with_columns(refs, near_ref, far_ref, rows, pair, act, total):
    count = refs[0].shape[0]
    for n, ref in enumerate(refs):
        adjacent_ref = far_ref if n >= 4 else near_ref

        def one(i, total, ref=ref, adjacent_ref=adjacent_ref, at=n % 4 * count * rows):
            start = pl.multiple_of(at + i * (pair * rows), pair * rows)
            return act(
                blocks_of(ref, i, pair, rows), adjacent_ref[:, pl.ds(start, pair * rows)], total
            )

        total = lax.fori_loop(0, count // pair, one, total, unroll=2)
    return total


def split_sums(total):
    high = total.astype(BF).astype(F32)
    low = (total - high).astype(BF).astype(F32)
    return jnp.concatenate([high, low])


def joined(parts):
    parts = parts.astype(F32)
    return parts[: EXTRA // 2] + parts[EXTRA // 2 :]


def put_sums(out_ref, width, parts):
    out_ref[width:, :LANES] = parts.astype(BF)
    if out_ref.shape[1] > LANES:
        out_ref[width:, LANES:] = jnp.zeros((EXTRA, out_ref.shape[1] - LANES), BF)


def pack_into(out_ref, turned, parts):
    width = turned.shape[0]
    out_ref[:width, :] = turned.astype(BF)
    if parts is not None:
        put_sums(out_ref, width, parts)


def add_up(values):
    values = list(values)
    while len(values) > 1:
        values = [values[i] + values[i + 1] for i in range(0, len(values), 2)]
    return values[0]


def cross(turned_refs, level_refs, start, stop, width, out):
    if len(level_refs) == 1:
        count = level_refs[0].shape[0]
        turned = [turned_refs[0].at[i] for i in range(count)]
        levels = [level_refs[0].at[i] for i in range(count)]
    else:
        turned, levels = turned_refs, level_refs
    total = None
    for i in range(0, len(levels), 2):
        left = jnp.concatenate([turned[i][:width, :], turned[i + 1][:width, :]], axis=1)
        right = jnp.concatenate([levels[i][:, start:stop], levels[i + 1][:, start:stop]])
        part = dot(left, right)
        total = part if total is None else total + part
    out(total)


def cross_kernel(width, count, *refs):
    turned_refs, level_refs, (send_ref,) = refs[:count], refs[count : 2 * count], refs[2 * count :]
    half = send_ref.shape[1]

    def out(value):
        send_ref[:width, :] = value.astype(BF)

    cross(turned_refs, level_refs, half, 2 * half, width, out)
    if send_ref.shape[0] > width:
        if count == 1:
            parts = [joined(turned_refs[0][i, width:, :]) for i in range(turned_refs[0].shape[0])]
        else:
            parts = [joined(ref[width:, :]) for ref in turned_refs]
        put_sums(send_ref, width, split_sums(add_up(parts)))


def keep_kernel(width, count, *refs):
    turned_refs, level_refs, (out_ref,) = refs[:count], refs[count : 2 * count], refs[2 * count :]

    def out(value):
        out_ref[...] = value

    cross(turned_refs, level_refs, 0, out_ref.shape[1], width, out)


def fold_kernel(kept_ref, send_ref, got_ref, own_ref, *piece_refs):
    width = kept_ref.shape[0]
    for k in range(4):
        cols = slice(k * LANES, (k + 1) * LANES)
        value = kept_ref[:, cols] + got_ref[:width, cols].astype(F32)
        if k == 0:
            own_ref[:width, :] = value
        else:
            piece_refs[k - 1][:width, :] = value.astype(BF)
    if own_ref.shape[0] > width:
        parts = split_sums(joined(send_ref[width:, :LANES]) + joined(got_ref[width:, :LANES]))
        own_ref[width:, :] = parts
        for piece_ref in piece_refs:
            put_sums(piece_ref, width, parts)


def spread_back(packed, levels, width):
    tall = packed.shape[0]
    if short_line():
        turned = [packed] + [pass_line(packed, k) for k in range(1, 4)]
    else:
        turned = [lax.all_gather(packed, "z", axis=0)]
    count = len(levels)
    half = levels[0].shape[-1] // 2
    work = 8 * width * LANES * half
    (send,) = run(
        functools.partial(cross_kernel, width, count),
        [shape((tall, half), BF)],
        [*turned, *levels],
        flops=work,
    )
    got = swap(send, 1)
    (kept,) = run(
        functools.partial(keep_kernel, width, count),
        [shape((width, half))],
        [*turned, *levels],
        flops=work,
    )
    own, *pieces = run(
        fold_kernel, [shape((tall, LANES))] + [shape((tall, LANES), BF)] * 3, [kept, send, got]
    )
    return [own] + [swap(pieces[k - 1], 2 * k) for k in range(1, 4)]


def line_total(refs, width):
    total = add_up(ref[:width, :].astype(F32) for ref in refs)
    if refs[0].shape[0] == width:
        return total, None
    return total, add_up(joined(ref[width:, :]) for ref in refs)


def wide(sums, row):
    return jnp.concatenate([sums[row : row + 1], sums[row + 1 : row + 2]], axis=1)


def put_wide(ref, row, value):
    ref[row : row + 1, :] = value[:, :LANES]
    ref[row + 1 : row + 2, :] = value[:, LANES:]


def layer_kernel(node_total, layer, near_ref, far_ref, weight_ref, norm_ref, *refs):
    refs, (out_ref, stats_ref) = refs[:8], refs[8:]
    count, tall, width = refs[0].shape
    rows = tall - EXTRA
    mean_value, inverse = moments(refs, node_total)
    stats_ref[0:1, :] = mean_value
    stats_ref[1:2, :] = inverse
    scale = norm_ref[2 * layer : 2 * layer + 1, :] * inverse
    start = norm_ref[2 * layer + 1 : 2 * layer + 2, :] - mean_value * scale
    low = weight_ref[...].astype(BF)

    def act(blocks, adjacent, total):
        hidden = []
        for value, centre in blocks:
            value = value * scale + (start + centre * scale)
            hidden.append((value * gelu_half(value)[0]).astype(BF))
        projected = dot(jnp.concatenate(hidden), low).astype(BF)
        return total + dot(adjacent, projected)

    total = jnp.zeros((rows, low.shape[1]), F32)
    centre_into(out_ref, with_columns(refs, near_ref, far_ref, rows, 2, act, total))


def slopes_kernel(layer, near_ref, far_ref, norm_ref, stats_ref, *refs):
    refs, out_ref = refs[:8], refs[8]
    count, tall, width = refs[0].shape
    rows = tall - EXTRA
    mean_value, inverse = stats_ref[0:1, :], stats_ref[1:2, :]
    gain = norm_ref[2 * layer : 2 * layer + 1, :]
    offset = norm_ref[2 * layer + 1 : 2 * layer + 2, :]
    out_ref[...] = jnp.zeros(out_ref.shape, F32)

    def act(blocks, adjacent, carry):
        slopes = []
        for value, centre in blocks:
            normed = value * inverse + (centre - mean_value) * inverse
            value = gain * normed + offset
            slope = gelu_slope(value, *gelu_half(value))
            slopes.append(jnp.concatenate([slope.astype(BF), (slope * normed).astype(BF)], axis=1))
        out_ref[...] += dot(adjacent, jnp.concatenate(slopes))
        return carry

    with_columns(refs, near_ref, far_ref, rows, 2, act, 0)


def head_low_of(weight_ref, tall_ref):
    tall_ref[...] = jnp.zeros(tall_ref.shape, F32)
    tall_ref[: weight_ref.shape[0], :] = weight_ref[...]
    return tall_ref[...].astype(BF)


def head_kernel(
    node_total, near_ref, far_ref, weight_ref, norm_ref, bias_ref, label_ref, mask_ref, *refs
):
    refs, (packed_ref, stats_ref, total_ref, sums_ref, tall_ref) = refs[:8], refs[8:]
    count, tall, width = refs[0].shape
    rows = tall - EXTRA
    classes = weight_ref.shape[0]
    mean_value, inverse = moments(refs, node_total)
    stats_ref[0:1, :] = mean_value
    stats_ref[1:2, :] = inverse
    gain, offset = norm_ref[2:3, :], norm_ref[3:4, :]
    low = head_low_of(weight_ref, tall_ref)
    total_ref[...] = jnp.zeros(total_ref.shape, F32)

    def act(blocks, adjacent, carry):
        hidden, slopes = [], []
        for value, centre in blocks:
            normed = value * inverse + (centre - mean_value) * inverse
            value = gain * normed + offset
            half, bend, square = gelu_half(value)
            slope = gelu_slope(value, half, bend, square)
            hidden.append((value * half).astype(BF))
            slopes.append(jnp.concatenate([slope.astype(BF), (slope * normed).astype(BF)], axis=1))
        headed = dot_turned(jnp.concatenate(hidden), low).astype(BF)
        both = jnp.concatenate([headed, jnp.concatenate(slopes)], axis=1)
        total_ref[...] += dot(adjacent, both)
        return carry

    with_columns(refs, near_ref, far_ref, rows, 2, act, 0)

    lane = lax.broadcasted_iota(jnp.int32, (rows, LANES), 1)
    sums_ref[...] = jnp.zeros(sums_ref.shape, F32)
    sums_ref[:1, :classes] = bias_ref[...]
    logits = jnp.where(lane < classes, total_ref[:, :LANES] + sums_ref[:1, :], -1e30)
    logits = logits - jnp.max(logits, axis=1, keepdims=True)
    raised = jnp.exp(logits)
    whole = jnp.sum(raised, axis=1, keepdims=True)
    label = jnp.broadcast_to(label_ref[...].astype(F32), (LANES, rows)).T
    onehot = jnp.where(lane.astype(F32) == label, 1.0, 0.0)
    weight = jnp.broadcast_to(mask_ref[...].astype(F32), (LANES, rows)).T
    losses = jnp.log(whole) - jnp.sum(onehot * logits, axis=1, keepdims=True)
    d_logits = (raised / whole - onehot) * weight
    d_low = d_logits.astype(BF)
    d_wide = dot(d_low, low)
    put_wide(sums_ref, 0, jnp.sum(d_wide * total_ref[:, LANES : LANES + width], axis=0, keepdims=True))
    put_wide(sums_ref, 2, jnp.sum(d_wide * total_ref[:, LANES + width :], axis=0, keepdims=True))
    sums_ref[4:5, :] = jnp.sum(d_logits, axis=0, keepdims=True)
    sums_ref[5:6, :] = jnp.sum(
        jnp.where(lane == 0, losses * weight, weight), axis=0, keepdims=True
    )
    pack_into(packed_ref, d_logits.T[:HEAD_ROWS], split_sums(sums_ref[...]))


def backward_norm(d_hidden, own_ref, stats_ref, norm_ref, layer, shift_grad, gain_grad, node_total):
    rows = own_ref.shape[0] - EXTRA
    mean_value, inverse = stats_ref[0:1, :], stats_ref[1:2, :]
    gain = norm_ref[2 * layer : 2 * layer + 1, :]
    centre = own_ref[rows:, :].astype(F32)[:1]
    normed = own_ref[:rows, :].astype(F32) * inverse + (centre - mean_value) * inverse
    value = gain * normed + norm_ref[2 * layer + 1 : 2 * layer + 2, :]
    half, bend, square = gelu_half(value)
    d_pre = d_hidden * gelu_slope(value, half, bend, square)
    d_summed = (gain * inverse) * (d_pre - (shift_grad + normed * gain_grad) / node_total)
    return d_summed, value * half


def second_kernel(
    node_total,
    head_ref,
    weight_ref,
    norm_ref,
    summed_ref,
    stats_ref,
    slopes_ref,
    *refs,
):
    refs, (packed_ref, grad_ref, out_ref, sums_ref, tall_ref) = refs[:4], refs[4:]
    headed, sums = line_total(refs, HEAD_ROWS)
    rows = headed.shape[1]
    each = 1.0 / sums[5:6, 1:2]
    headed = headed * each
    put_row = lax.broadcasted_iota(jnp.int32, sums.shape, 0)
    out_ref[...] = jnp.where(put_row == 5, sums, sums * each)
    turned_back = jnp.concatenate([headed, jnp.zeros((LANES - HEAD_ROWS, rows), F32)]).T
    d_hidden = dot(turned_back.astype(BF), head_low_of(head_ref, tall_ref))
    d_summed, hidden = backward_norm(
        d_hidden, summed_ref, stats_ref, norm_ref, 1, wide(sums, 0) * each, wide(sums, 2) * each, node_total
    )
    grad_ref[...] = dot(headed.astype(BF), hidden.astype(BF))
    d_wide = dot_turned(d_summed.astype(BF), weight_ref[...].astype(BF))
    width = d_wide.shape[1]
    put_wide(sums_ref, 0, jnp.sum(d_wide * slopes_ref[:, :width], axis=0, keepdims=True))
    put_wide(sums_ref, 2, jnp.sum(d_wide * slopes_ref[:, width:], axis=0, keepdims=True))
    sums_ref[4:8, :] = jnp.zeros((4, LANES), F32)
    pack_into(packed_ref, d_summed.T, split_sums(sums_ref[...]))


def mix_kernel(near_ref, far_ref, *refs):
    outs = 1 if len(refs) == 2 else 4
    level_refs, out_refs = refs[:outs], refs[outs:]

    def one(level_ref):
        total = None
        for n in range(0, 8, 2):
            ref = far_ref if n >= 4 else near_ref
            left = jnp.concatenate([ref[n % 4], ref[n % 4 + 1]], axis=1)
            part = dot_turned(left, level_ref[:, n * TILE : (n + 2) * TILE])
            total = part if total is None else total + part
        return total

    if outs == 1:

        def step(i, carry):
            out_refs[0][i] = one(level_refs[0].at[i])
            return carry

        lax.fori_loop(0, level_refs[0].shape[0], step, 0)
        return
    for level_ref, out_ref in zip(level_refs, out_refs, strict=True):
        out_ref[...] = one(level_ref).astype(out_ref.dtype)


def first_kernel(node_total, inputs_tall, mixes, weight_ref, norm_ref, summed_ref, stats_ref, head_ref, *refs):
    mix_refs, refs = refs[:mixes], refs[mixes:]
    refs, (away_ref, kept_ref, out_ref, pile_ref) = refs[:4], refs[4:]
    width = weight_ref.shape[1]
    d_projected, sums = line_total(refs, width)
    out_ref[...] = sums
    d_projected = d_projected.T.astype(BF)
    d_hidden = dot_turned(d_projected, weight_ref[...].astype(BF))
    d_summed, hidden = backward_norm(
        d_hidden, summed_ref, stats_ref, norm_ref, 0, wide(sums, 0), wide(sums, 2), node_total
    )
    mixed = add_up(ref[...].astype(F32) for ref in mix_refs).astype(BF)
    pile_ref[...] = jnp.zeros(pile_ref.shape, F32)
    pile_ref[: mixed.shape[0], :] = dot(mixed, d_summed.astype(BF))
    at = inputs_tall
    pile_ref[at : at + width, :] = dot(hidden.T.astype(BF), d_projected)
    at += width
    pile_ref[at : at + HEAD_ROWS, :] = head_ref[...]
    half = away_ref.shape[0]
    core = lax.axis_index("c")
    away_ref[...] = pile_ref[pl.ds(pl.multiple_of((1 - core) * half, half), half), :].astype(BF)
    kept_ref[...] = pile_ref[pl.ds(pl.multiple_of(core * half, half), half), :]


def pile_core_kernel(kept_ref, got_ref, own_ref, *piece_refs):
    size = own_ref.shape[0]
    here = 2 * lax.axis_index("y") + lax.axis_index("x")
    for k in range(4):
        at = pl.ds(pl.multiple_of(jnp.bitwise_xor(here, k) * size, size), size)
        value = kept_ref[at, :] + got_ref[at, :].astype(F32)
        if k == 0:
            own_ref[...] = value
        else:
            piece_refs[k - 1][...] = value.astype(BF)


def pile_sum_kernel(own_ref, *refs):
    parts = [own_ref, *refs[:3]]
    refs[3][...] = add_up(ref[...].astype(F32) for ref in parts).astype(refs[3].dtype)


def update_kernel(inputs_tall, *refs):
    pieces, refs = refs[:8], refs[8:]
    inputs, outs, pile_ref = refs[:9], refs[9:18], refs[18]
    size, width = pieces[0].shape
    here = 2 * lax.axis_index("y") + lax.axis_index("x")
    core = lax.axis_index("c")
    for n, ref in enumerate(pieces):
        at = (jnp.bitwise_xor(core, n // 4) * 4 + jnp.bitwise_xor(here, n % 4)) * size
        pile_ref[pl.ds(pl.multiple_of(at, size), size), :] = ref[...].astype(F32)
    tall = inputs[0].shape[0]
    grads = (
        pile_ref[:tall, :],
        pile_ref[inputs_tall : inputs_tall + width, :],
        pile_ref[inputs_tall + width : inputs_tall + width + inputs[6].shape[0], :],
    )
    for n in range(3):
        weight, first, second = (ref[...] for ref in inputs[3 * n : 3 * n + 3])
        results = adamw(weight, grads[n], first, second, RATE_MATRIX)
        for ref, value in zip(outs[3 * n : 3 * n + 3], results, strict=True):
            ref[...] = value


def sum_pile(away, kept):
    size = away.shape[0] // 4
    width = away.shape[1]
    got = swap(away, 1)
    own, *pieces = run(
        pile_core_kernel, [shape((size, width))] + [shape((size, width), BF)] * 3, [kept, got]
    )
    got = [swap(pieces[k - 1], 2 * k) for k in range(1, 4)]
    if short_line():
        (shard,) = run(pile_sum_kernel, [shape((size, width), BF)], [own, *got])
        got = [pass_line(shard, k) for k in range(1, 4)]
        (shard,) = run(pile_sum_kernel, [shape((size, width), BF)], [shard, *got])
    else:
        (shard,) = run(pile_sum_kernel, [shape((size, width))], [own, *got])
        shard = lax.psum(shard, "z").astype(BF)
    pieces = [shard] + [swap(shard, 2 * k) for k in range(1, 4)]
    return pieces + [swap(piece, 1) for piece in pieces]


def first_sum_kernel(near_ref, far_ref, *refs):
    refs, out_ref = refs[:8], refs[8]
    count, rows, width = refs[0].shape
    total = jnp.zeros((rows, width), F32)
    for n, ref in enumerate(refs):
        adjacent_ref = far_ref if n >= 4 else near_ref
        at = n % 4 * count * rows
        total = total + dot(
            adjacent_ref[:, at : at + count * rows], ref[...].reshape(count * rows, width)
        )
    centre_into(out_ref, total)


def per_device(
    features,
    adjacency,
    tile_mask,
    labels,
    train_mask,
    w_first,
    w_second,
    w_head,
    norm_params,
    head_bias,
    m_first,
    m_second,
    m_head,
    m_norms,
    m_bias,
    v_first,
    v_second,
    v_head,
    v_norms,
    v_bias,
):
    rows, node_total = adjacency.shape
    inputs, hidden = w_first.shape
    classes = w_head.shape[1]
    half = node_total // 2
    length = lax.axis_size("z")
    tall = rows + EXTRA
    inputs_tall = -(-inputs // EXTRA) * EXTRA
    head_turned = w_head.T
    work = 2 * rows * node_total * hidden

    if short_line():
        level_shapes = [shape((rows, 8 * rows), BF)] * 4
    else:
        level_shapes = [shape((length, rows, 8 * rows), BF)]
    near, far, *levels = run(
        arrange_kernel,
        [shape((rows, half), BF)] * 2 + level_shapes,
        [tile_mask, adjacency],
        scalars=1,
    )

    projected = dot(features, w_first.astype(BF)).astype(BF)
    turned = features.T
    turned = jnp.stack([turned] + [swap(turned, 2 * k) for k in range(1, 4)])
    if short_line():
        around, passed, (turned,) = gather_all(
            projected, [(levels[1], 1), (levels[2], 2)], [turned]
        )
        levels[1:3] = passed
    else:
        around, *unused = gather_all(projected)
        levels = [lax.all_to_all(levels[0], "z", 0, 0)]
    (summed_one,) = run(
        first_sum_kernel, [shape((tall, hidden), BF)], [near, far, *around], flops=work
    )
    if short_line():
        around, levels[3:], unused = gather_all(summed_one, [(levels[3], 3)])
    else:
        around, *unused = gather_all(summed_one)
    summed_two, stats_one = run(
        functools.partial(layer_kernel, node_total, 0),
        [shape((tall, hidden), BF), shape((8, hidden))],
        [near, far, w_second, norm_params, *around],
        flops=3 * work,
    )
    (slopes_one,) = run(
        functools.partial(slopes_kernel, 0),
        [shape((rows, 2 * hidden))],
        [near, far, norm_params, stats_one, *around],
        flops=3 * work,
    )
    if short_line():
        mixed_shapes = [shape((inputs, rows))] + [shape((inputs, rows), BF)] * 3
    else:
        mixed_shapes = [shape((length, inputs, rows))]
    mixed = run(
        mix_kernel, mixed_shapes, [turned, swap(turned, 1), *levels], flops=2 * work
    )
    if short_line():
        around, passed, unused = gather_all(summed_two, [(mixed[k], k) for k in range(1, 4)])
        mixed = [mixed[0], *passed]
    else:
        around, *unused = gather_all(summed_two)
        mixed = [lax.psum_scatter(mixed[0], "z", scatter_dimension=0)]
    packed, stats_two = run(
        functools.partial(head_kernel, node_total),
        [shape((HEAD_ROWS + EXTRA, rows), BF), shape((8, hidden))],
        [
            near,
            far,
            head_turned,
            norm_params,
            head_bias[None],
            labels[None],
            train_mask[None],
            *around,
        ],
        scratch=[
            pltpu.VMEM((rows, LANES + 2 * hidden), F32),
            pltpu.VMEM((8, LANES), F32),
            pltpu.VMEM((LANES, hidden), F32),
        ],
        flops=4 * work,
    )

    packed, head_grad, sums_two = run(
        functools.partial(second_kernel, node_total),
        [shape((hidden + EXTRA, rows), BF), shape((HEAD_ROWS, hidden)), shape((8, LANES))],
        [
            head_turned,
            w_second,
            norm_params,
            summed_two,
            stats_two,
            slopes_one,
            *spread_back(packed, levels, HEAD_ROWS),
        ],
        scratch=[pltpu.VMEM((8, LANES), F32), pltpu.VMEM((LANES, hidden), F32)],
        flops=work // 4,
    )
    size = -(-(inputs_tall + hidden + HEAD_ROWS) // (8 * EXTRA)) * EXTRA
    away, kept, sums_one = run(
        functools.partial(first_kernel, node_total, inputs_tall, len(mixed)),
        [shape((4 * size, hidden), BF), shape((4 * size, hidden)), shape((8, LANES))],
        [
            w_second,
            norm_params,
            summed_one,
            stats_one,
            head_grad,
            *mixed,
            *spread_back(packed, levels, hidden),
        ],
        scratch=[pltpu.VMEM((8 * size, hidden), F32)],
        flops=work,
    )
    matrices = (
        *(w_first, m_first, v_first, w_second, m_second, v_second),
        *(head_turned, m_head.T, v_head.T),
    )
    updated = run(
        functools.partial(update_kernel, inputs_tall),
        [shape(block.shape) for block in matrices],
        [*sum_pile(away, kept), *matrices],
        scratch=[pltpu.VMEM((8 * size, hidden), F32)],
    )
    updated = [*updated[:6], *(block.T for block in updated[6:])]

    def pair(sums):
        return sums[2:4].reshape(1, hidden), sums[0:2].reshape(1, hidden)

    norm_grad = jnp.concatenate([*pair(sums_one), *pair(sums_two)])
    norms = adamw(norm_params, norm_grad, m_norms, v_norms, RATE_SMALL)
    bias = adamw(head_bias, sums_two[4, :classes], m_bias, v_bias, RATE_SMALL)
    loss_sum, train_count = sums_two[5, 0], sums_two[5, 1]
    return (
        loss_sum,
        train_count,
        *(
            part
            for n in range(3)
            for part in (updated[n], updated[3 + n], updated[6 + n], norms[n], bias[n])
        ),
    )


def solution(mesh):
    wide_mesh = Mesh(mesh.devices.reshape(-1, 2, 2, 2), EVERY)
    split = (P(EVERY, None),) * 3 + (P(EVERY),) * 2
    return jax.shard_map(
        per_device,
        mesh=wide_mesh,
        in_specs=split + (P(),) * 15,
        out_specs=(P(),) * 17,
        check_vma=False,
    )
```

```python
import functools
import math

import jax
import jax.numpy as jnp
from jax import lax
from jax.experimental import pallas as pl
from jax.experimental.pallas import tpu as pltpu
from jax.sharding import Mesh
from jax.sharding import PartitionSpec as P

TILE = 128
STEP = 10
EPS_NORM = 1e-05
EPS_ADAM = 1e-08
BETA_ONE = 0.9
BETA_TWO = 0.999
DECAY = 0.01
RATE_MATRIX = 0.03
RATE_SMALL = 0.3

BF = jnp.bfloat16
F32 = jnp.float32
PLANE = ("y", "x", "c")
EVERY = ("z", "y", "x", "c")
LANES = 128
HEAD_ROWS = 48
EXTRA = 16
ROOT = math.sqrt(2.0 / math.pi)
BEND = 0.044715


def adamw(weight, gradient, first, second, rate):
    first_new = BETA_ONE * first + (1.0 - BETA_ONE) * gradient
    second_new = BETA_TWO * second + (1.0 - BETA_TWO) * gradient * gradient
    scaled = (
        first_new
        / (1.0 - BETA_ONE**STEP)
        / (jnp.sqrt(second_new / (1.0 - BETA_TWO**STEP)) + EPS_ADAM)
    )
    return (weight - rate * (scaled + DECAY * weight), first_new, second_new)


def dot(left, right):
    return jnp.dot(left, right, preferred_element_type=F32)


def dot_turned(left, right):
    return lax.dot_general(left, right, (((1,), (1,)), ((), ())), preferred_element_type=F32)


def shape(dims, kind=F32):
    return jax.ShapeDtypeStruct(dims, kind)


def run(body, outs, ins, scratch=(), flops=0, scalars=0):
    held = sum(math.prod(a.shape[:-1]) * max(a.shape[-1], LANES) * a.dtype.itemsize for a in (*ins, *outs))
    limit = min(60 << 20, 2 * held + (8 << 20))
    return pl.pallas_call(
        body,
        out_shape=tuple(outs),
        in_specs=[pl.BlockSpec(memory_space=pltpu.SMEM)] * scalars
        + [pl.BlockSpec(memory_space=pltpu.VMEM)] * (len(ins) - scalars),
        out_specs=tuple(pl.BlockSpec(memory_space=pltpu.VMEM) for unused in outs),
        scratch_shapes=list(scratch),
        compiler_params=pltpu.CompilerParams(vmem_limit_bytes=limit),
        cost_estimate=pl.CostEstimate(flops=flops, bytes_accessed=held, transcendentals=0),
    )(*ins)


def swap(block, mask):
    return lax.ppermute(block, PLANE, [(i, i ^ mask) for i in range(8)])


def pass_line(block, mask):
    return lax.ppermute(block, "z", [(i, i ^ mask) for i in range(4)])


def short_line():
    return lax.axis_size("z") == 4


def after(block, *others):
    return lax.optimization_barrier((block, *others))[0]


def gather_all(block, beside=(), within=()):
    if short_line():
        line = [block] + [pass_line(block, k) for k in range(1, 4)]
        line = jnp.stack(line)
    else:
        line = lax.all_gather(block, "z", axis=0)
    passed = [pass_line(after(part, line), mask) for part, mask in beside]
    lines = [line] + [swap(line, 2 * k) for k in range(1, 4)]
    if passed or within:
        lines[3], *rest = lax.optimization_barrier((lines[3], *passed, *within))
        passed, within = rest[: len(passed)], rest[len(passed) :]
    return lines + [swap(line, 1) for line in lines], passed, within


def arrange_kernel(
    mask_ref, values_ref, label_ref, train_ref, bias_ref, near_ref, far_ref, notes_ref, *level_refs
):
    notes_ref[...] = jnp.zeros(notes_ref.shape, F32)
    notes_ref[0:1, :] = label_ref[...].astype(F32)
    notes_ref[1:2, :] = train_ref[...].astype(F32)
    notes_ref[2:3, : bias_ref.shape[1]] = bias_ref[...]
    half = near_ref.shape[1] // TILE
    lines = half // 4
    here = 4 * lax.axis_index("y") + 2 * lax.axis_index("x") + lax.axis_index("c")
    level = lax.axis_index("z") if short_line() else 0

    for core, out_ref in ((0, near_ref), (1, far_ref)):
        for place in range(4):

            def one(step, carry, core=core, place=place, out_ref=out_ref):
                source = jnp.bitwise_xor(step, level) * 8 + jnp.bitwise_xor(place * 2 + core, here)
                keep = mask_ref[0, source].astype(F32).astype(BF)
                block = values_ref[:, pl.ds(pl.multiple_of(source * TILE, TILE), TILE)] * keep
                at = pl.multiple_of((place * lines + step) * TILE, TILE)
                out_ref[:, pl.ds(at, TILE)] = block
                cols = slice((core * 4 + place) * TILE, (core * 4 + place + 1) * TILE)
                if len(level_refs) == 1:
                    level_refs[0][step, :, cols] = block
                else:
                    level_refs[step][:, cols] = block
                return carry

            if len(level_refs) == 1:
                lax.fori_loop(0, lines, one, 0)
            else:
                for step in range(lines):
                    one(step, 0)


def centre_into(out_ref, summed):
    rows = summed.shape[0]
    centre = (jnp.sum(summed, axis=0, keepdims=True) / rows).astype(BF).astype(F32)
    out_ref[:rows, :] = (summed - centre).astype(BF)
    out_ref[rows:, :] = jnp.broadcast_to(centre, (EXTRA, summed.shape[1])).astype(BF)


def block_at(ref, i, rows):
    return ref[i, :rows, :].astype(F32), ref[i, rows:, :].astype(F32)[:1]


def block_loop(ref, pair, body, carry):
    if ref.shape[0] > 4:
        return lax.fori_loop(
            0, ref.shape[0] // pair, lambda i, carry: body(i * pair, carry), carry
        )
    for i in range(0, 4, pair):
        carry = body(i, carry)
    return carry


def moments(refs, rows, node_total):
    width = refs[0].shape[-1]
    pivot = block_at(refs[0], 0, rows)[1]
    zero = jnp.zeros((8, width), F32)
    sums = (zero, zero)
    for ref in refs:

        def one(i, carry, ref=ref):
            total, square = carry
            value, centre = block_at(ref, i, rows)
            value = value.reshape(rows // 8, 8, width)
            part = jnp.sum(value, axis=0)
            away = centre - pivot
            each = away * (rows // 8)
            return (
                total + part + each,
                square + jnp.sum(value * value, axis=0) + away * (2.0 * part + each),
            )

        sums = block_loop(ref, 1, one, sums)
    shift = jnp.sum(sums[0], axis=0, keepdims=True) / node_total
    variance = jnp.sum(sums[1], axis=0, keepdims=True) / node_total - shift * shift
    return pivot + shift, lax.rsqrt(jnp.maximum(variance, 0.0) + EPS_NORM)


def gelu_half(value):
    square = value * value
    bend = jnp.tanh(value * (ROOT + (ROOT * BEND) * square))
    return 0.5 + 0.5 * bend, square


def gelu_slope(value, half, square):
    return half + (value * half) * (1.0 - half) * (2 * ROOT + (6 * ROOT * BEND) * square)


def with_columns(refs, near_ref, far_ref, act, total):
    rows, columns = near_ref.shape
    for n, ref in enumerate(refs):
        adjacent_ref = far_ref if n >= 4 else near_ref

        def one(i, total, ref=ref, adjacent_ref=adjacent_ref, at=n % 4 * (columns // 4)):
            start = at + i * rows
            if not isinstance(start, int):
                start = pl.multiple_of(start, 4 * rows)
            blocks = [block_at(ref, i + j, rows) for j in range(4)]
            return act(blocks, adjacent_ref[:, pl.ds(start, 4 * rows)], total)

        total = block_loop(ref, 4, one, total)
    return total


def split_sums(total):
    high = total.astype(BF).astype(F32)
    low = (total - high).astype(BF).astype(F32)
    return jnp.concatenate([high, low])


def joined(parts):
    parts = parts.astype(F32)
    return parts[: EXTRA // 2] + parts[EXTRA // 2 :]


def put_sums(out_ref, width, parts):
    out_ref[width:, :LANES] = parts.astype(BF)
    if out_ref.shape[1] > LANES:
        out_ref[width:, LANES:] = jnp.zeros((EXTRA, out_ref.shape[1] - LANES), BF)


def pack_into(out_ref, turned, parts):
    width = turned.shape[0]
    out_ref[:width, :] = turned.astype(BF)
    if parts is not None:
        put_sums(out_ref, width, parts)


def add_up(values):
    values = list(values)
    while len(values) > 1:
        values = [values[i] + values[i + 1] for i in range(0, len(values), 2)]
    return values[0]


def cross(turned_refs, level_refs, start, stop, width, out):
    if len(level_refs) == 1:
        count = level_refs[0].shape[0]
        turned = [turned_refs[0].at[i] for i in range(count)]
        levels = [level_refs[0].at[i] for i in range(count)]
    else:
        turned, levels = turned_refs, level_refs
    total = None
    for i in range(0, len(levels), 2):
        left = jnp.concatenate([turned[i][:width, :], turned[i + 1][:width, :]], axis=1)
        right = jnp.concatenate([levels[i][:, start:stop], levels[i + 1][:, start:stop]])
        part = dot(left, right)
        total = part if total is None else total + part
    out(total)


def cross_kernel(width, count, *refs):
    turned_refs, level_refs, (send_ref,) = refs[:count], refs[count : 2 * count], refs[2 * count :]
    half = send_ref.shape[1]

    def out(value):
        send_ref[:width, :] = value.astype(BF)

    cross(turned_refs, level_refs, half, 2 * half, width, out)
    if send_ref.shape[0] > width:
        if count == 1:
            parts = [joined(turned_refs[0][i, width:, :]) for i in range(turned_refs[0].shape[0])]
        else:
            parts = [joined(ref[width:, :]) for ref in turned_refs]
        put_sums(send_ref, width, split_sums(add_up(parts)))


def keep_kernel(width, count, *refs):
    turned_refs, level_refs, (out_ref,) = refs[:count], refs[count : 2 * count], refs[2 * count :]

    def out(value):
        out_ref[...] = value

    cross(turned_refs, level_refs, 0, out_ref.shape[1], width, out)


def fold_kernel(kept_ref, send_ref, got_ref, own_ref, *piece_refs):
    width = kept_ref.shape[0]
    for k in range(4):
        cols = slice(k * LANES, (k + 1) * LANES)
        value = kept_ref[:, cols] + got_ref[:width, cols].astype(F32)
        if k == 0:
            own_ref[:width, :] = value
        else:
            piece_refs[k - 1][:width, :] = value.astype(BF)
    if own_ref.shape[0] > width:
        parts = split_sums(joined(send_ref[width:, :LANES]) + joined(got_ref[width:, :LANES]))
        own_ref[width:, :] = parts
        for piece_ref in piece_refs:
            put_sums(piece_ref, width, parts)


def spread_back(packed, levels, width):
    tall = packed.shape[0]
    if short_line():
        turned = [packed] + [pass_line(packed, k) for k in range(1, 4)]
    else:
        turned = [lax.all_gather(packed, "z", axis=0)]
    count = len(levels)
    half = levels[0].shape[-1] // 2
    work = 8 * width * LANES * half
    (send,) = run(
        functools.partial(cross_kernel, width, count),
        [shape((tall, half), BF)],
        [*turned, *levels],
        flops=work,
    )
    got = swap(send, 1)
    (kept,) = run(
        functools.partial(keep_kernel, width, count),
        [shape((width, half))],
        [*turned, *levels],
        flops=work,
    )
    own, *pieces = run(
        fold_kernel, [shape((tall, LANES))] + [shape((tall, LANES), BF)] * 3, [kept, send, got]
    )
    return [own] + [swap(pieces[k - 1], 2 * k) for k in range(1, 4)]


def line_total(refs, width):
    total = add_up(ref[:width, :].astype(F32) for ref in refs)
    if refs[0].shape[0] == width:
        return total, None
    return total, add_up(joined(ref[width:, :]) for ref in refs)


def wide(sums, row):
    return jnp.concatenate([sums[row : row + 1], sums[row + 1 : row + 2]], axis=1)


def put_wide(ref, row, value):
    ref[row : row + 1, :] = value[:, :LANES]
    ref[row + 1 : row + 2, :] = value[:, LANES:]


def layer_kernel(node_total, layer, near_ref, far_ref, weight_ref, norm_ref, *refs):
    refs, (out_ref, stats_ref) = refs[:8], refs[8:]
    rows, width = near_ref.shape[0], refs[0].shape[-1]
    mean_value, inverse = moments(refs, rows, node_total)
    stats_ref[0:1, :] = mean_value
    stats_ref[1:2, :] = inverse
    scale = norm_ref[2 * layer : 2 * layer + 1, :] * inverse
    start = norm_ref[2 * layer + 1 : 2 * layer + 2, :] - mean_value * scale
    low = weight_ref[...].astype(BF)

    def act(blocks, adjacent, total):
        hidden = []
        for value, centre in blocks:
            value = value * scale + (start + centre * scale)
            hidden.append((value * gelu_half(value)[0]).astype(BF))
        projected = dot(jnp.concatenate(hidden), low).astype(BF)
        return total + dot(adjacent, projected)

    total = jnp.zeros((rows, low.shape[1]), F32)
    centre_into(out_ref, with_columns(refs, near_ref, far_ref, act, total))


def slopes_kernel(layer, near_ref, far_ref, norm_ref, stats_ref, *refs):
    refs, out_ref = refs[:8], refs[8]
    mean_value, inverse = stats_ref[0:1, :], stats_ref[1:2, :]
    gain = norm_ref[2 * layer : 2 * layer + 1, :]
    offset = norm_ref[2 * layer + 1 : 2 * layer + 2, :]
    out_ref[...] = jnp.zeros(out_ref.shape, F32)

    def act(blocks, adjacent, carry):
        slopes = []
        for value, centre in blocks:
            normed = value * inverse + (centre - mean_value) * inverse
            value = gain * normed + offset
            slope = gelu_slope(value, *gelu_half(value))
            slopes.append(jnp.concatenate([slope.astype(BF), (slope * normed).astype(BF)], axis=1))
        out_ref[...] += dot(adjacent, jnp.concatenate(slopes))
        return carry

    with_columns(refs, near_ref, far_ref, act, 0)


def head_low_of(weight_ref, tall_ref):
    tall_ref[...] = jnp.zeros(tall_ref.shape, F32)
    tall_ref[: weight_ref.shape[0], :] = weight_ref[...]
    return tall_ref[...].astype(BF)


def head_kernel(node_total, near_ref, far_ref, weight_ref, norm_ref, notes_ref, *refs):
    refs, (packed_ref, stats_ref, total_ref, sums_ref, tall_ref) = refs[:8], refs[8:]
    rows, width = near_ref.shape[0], refs[0].shape[-1]
    classes = weight_ref.shape[0]
    mean_value, inverse = moments(refs, rows, node_total)
    stats_ref[0:1, :] = mean_value
    stats_ref[1:2, :] = inverse
    gain, offset = norm_ref[2:3, :], norm_ref[3:4, :]
    low = head_low_of(weight_ref, tall_ref)
    total_ref[...] = jnp.zeros(total_ref.shape, F32)

    def act(blocks, adjacent, carry):
        hidden, slopes = [], []
        for value, centre in blocks:
            normed = value * inverse + (centre - mean_value) * inverse
            value = gain * normed + offset
            half, square = gelu_half(value)
            slope = gelu_slope(value, half, square)
            hidden.append((value * half).astype(BF))
            slopes.append(jnp.concatenate([slope.astype(BF), (slope * normed).astype(BF)], axis=1))
        headed = dot_turned(jnp.concatenate(hidden), low).astype(BF)
        both = jnp.concatenate([headed, jnp.concatenate(slopes)], axis=1)
        total_ref[...] += dot(adjacent, both)
        return carry

    with_columns(refs, near_ref, far_ref, act, 0)

    lane = lax.broadcasted_iota(jnp.int32, (rows, LANES), 1)
    sums_ref[...] = jnp.zeros(sums_ref.shape, F32)
    logits = jnp.where(lane < classes, total_ref[:, :LANES] + notes_ref[2:3, :], -1e30)
    logits = logits - jnp.max(logits, axis=1, keepdims=True)
    raised = jnp.exp(logits)
    whole = jnp.sum(raised, axis=1, keepdims=True)
    label = jnp.broadcast_to(notes_ref[0:1, :], (LANES, rows)).T
    onehot = jnp.where(lane.astype(F32) == label, 1.0, 0.0)
    weight = jnp.broadcast_to(notes_ref[1:2, :], (LANES, rows)).T
    losses = jnp.log(whole) - jnp.sum(onehot * logits, axis=1, keepdims=True)
    d_logits = (raised / whole - onehot) * weight
    d_low = d_logits.astype(BF)
    d_wide = dot(d_low, low)
    put_wide(sums_ref, 0, jnp.sum(d_wide * total_ref[:, LANES : LANES + width], axis=0, keepdims=True))
    put_wide(sums_ref, 2, jnp.sum(d_wide * total_ref[:, LANES + width :], axis=0, keepdims=True))
    sums_ref[4:5, :] = jnp.sum(d_logits, axis=0, keepdims=True)
    sums_ref[5:6, :] = jnp.sum(
        jnp.where(lane == 0, losses * weight, weight), axis=0, keepdims=True
    )
    pack_into(packed_ref, d_logits.T[:HEAD_ROWS], split_sums(sums_ref[...]))


def backward_norm(d_hidden, own_ref, stats_ref, norm_ref, layer, shift_grad, gain_grad, node_total):
    rows = own_ref.shape[0] - EXTRA
    mean_value, inverse = stats_ref[0:1, :], stats_ref[1:2, :]
    gain = norm_ref[2 * layer : 2 * layer + 1, :]
    centre = own_ref[rows:, :].astype(F32)[:1]
    normed = own_ref[:rows, :].astype(F32) * inverse + (centre - mean_value) * inverse
    value = gain * normed + norm_ref[2 * layer + 1 : 2 * layer + 2, :]
    half, square = gelu_half(value)
    d_pre = d_hidden * gelu_slope(value, half, square)
    d_summed = (gain * inverse) * (d_pre - (shift_grad + normed * gain_grad) / node_total)
    return d_summed, value * half


def second_kernel(
    node_total,
    head_ref,
    weight_ref,
    norm_ref,
    summed_ref,
    stats_ref,
    slopes_ref,
    *refs,
):
    refs, (packed_ref, grad_ref, out_ref, sums_ref, tall_ref) = refs[:4], refs[4:]
    headed, sums = line_total(refs, HEAD_ROWS)
    rows = headed.shape[1]
    each = 1.0 / sums[5:6, 1:2]
    headed = headed * each
    put_row = lax.broadcasted_iota(jnp.int32, sums.shape, 0)
    out_ref[...] = jnp.where(put_row == 5, sums, sums * each)
    turned_back = jnp.concatenate([headed, jnp.zeros((LANES - HEAD_ROWS, rows), F32)]).T
    d_hidden = dot(turned_back.astype(BF), head_low_of(head_ref, tall_ref))
    d_summed, hidden = backward_norm(
        d_hidden, summed_ref, stats_ref, norm_ref, 1, wide(sums, 0) * each, wide(sums, 2) * each, node_total
    )
    grad_ref[...] = dot(headed.astype(BF), hidden.astype(BF))
    d_wide = dot_turned(d_summed.astype(BF), weight_ref[...].astype(BF))
    width = d_wide.shape[1]
    put_wide(sums_ref, 0, jnp.sum(d_wide * slopes_ref[:, :width], axis=0, keepdims=True))
    put_wide(sums_ref, 2, jnp.sum(d_wide * slopes_ref[:, width:], axis=0, keepdims=True))
    sums_ref[4:8, :] = jnp.zeros((4, LANES), F32)
    pack_into(packed_ref, d_summed.T, split_sums(sums_ref[...]))


def mix_kernel(near_ref, far_ref, *refs):
    outs = 1 if len(refs) == 2 else 4
    level_refs, out_refs = refs[:outs], refs[outs:]

    def one(level_ref):
        total = None
        for n in range(0, 8, 2):
            ref = far_ref if n >= 4 else near_ref
            left = jnp.concatenate([ref[n % 4], ref[n % 4 + 1]], axis=1)
            part = dot_turned(left, level_ref[:, n * TILE : (n + 2) * TILE])
            total = part if total is None else total + part
        return total

    if outs == 1:

        def step(i, carry):
            out_refs[0][i] = one(level_refs[0].at[i])
            return carry

        lax.fori_loop(0, level_refs[0].shape[0], step, 0)
        return
    for level_ref, out_ref in zip(level_refs, out_refs, strict=True):
        out_ref[...] = one(level_ref).astype(out_ref.dtype)


def first_kernel(node_total, inputs_tall, mixes, weight_ref, norm_ref, summed_ref, stats_ref, head_ref, *refs):
    mix_refs, refs = refs[:mixes], refs[mixes:]
    refs, (away_ref, kept_ref, out_ref, pile_ref) = refs[:4], refs[4:]
    width = weight_ref.shape[1]
    d_projected, sums = line_total(refs, width)
    out_ref[...] = sums
    d_projected = d_projected.T.astype(BF)
    d_hidden = dot_turned(d_projected, weight_ref[...].astype(BF))
    d_summed, hidden = backward_norm(
        d_hidden, summed_ref, stats_ref, norm_ref, 0, wide(sums, 0), wide(sums, 2), node_total
    )
    mixed = add_up(ref[...].astype(F32) for ref in mix_refs).astype(BF)
    pile_ref[...] = jnp.zeros(pile_ref.shape, F32)
    pile_ref[: mixed.shape[0], :] = dot(mixed, d_summed.astype(BF))
    at = inputs_tall
    pile_ref[at : at + width, :] = dot(hidden.T.astype(BF), d_projected)
    at += width
    pile_ref[at : at + HEAD_ROWS, :] = head_ref[...]
    half = away_ref.shape[0]
    core = lax.axis_index("c")
    away_ref[...] = pile_ref[pl.ds(pl.multiple_of((1 - core) * half, half), half), :].astype(BF)
    kept_ref[...] = pile_ref[pl.ds(pl.multiple_of(core * half, half), half), :]


def pile_core_kernel(kept_ref, got_ref, own_ref, *piece_refs):
    size = own_ref.shape[0]
    here = 2 * lax.axis_index("y") + lax.axis_index("x")
    for k in range(4):
        at = pl.ds(pl.multiple_of(jnp.bitwise_xor(here, k) * size, size), size)
        value = kept_ref[at, :] + got_ref[at, :].astype(F32)
        if k == 0:
            own_ref[...] = value
        else:
            piece_refs[k - 1][...] = value.astype(BF)


def pile_sum_kernel(own_ref, *refs):
    parts = [own_ref, *refs[:3]]
    refs[3][...] = add_up(ref[...].astype(F32) for ref in parts).astype(refs[3].dtype)


def update_kernel(inputs_tall, *refs):
    pieces, refs = refs[:8], refs[8:]
    inputs, outs, pile_ref = refs[:9], refs[9:18], refs[18]
    size, width = pieces[0].shape
    here = 2 * lax.axis_index("y") + lax.axis_index("x")
    core = lax.axis_index("c")
    for n, ref in enumerate(pieces):
        at = (jnp.bitwise_xor(core, n // 4) * 4 + jnp.bitwise_xor(here, n % 4)) * size
        pile_ref[pl.ds(pl.multiple_of(at, size), size), :] = ref[...].astype(F32)
    tall = inputs[0].shape[0]
    grads = (
        pile_ref[:tall, :],
        pile_ref[inputs_tall : inputs_tall + width, :],
        pile_ref[inputs_tall + width : inputs_tall + width + inputs[6].shape[0], :],
    )
    for n in range(3):
        weight, first, second = (ref[...] for ref in inputs[3 * n : 3 * n + 3])
        results = adamw(weight, grads[n], first, second, RATE_MATRIX)
        for ref, value in zip(outs[3 * n : 3 * n + 3], results, strict=True):
            ref[...] = value


def sum_pile(away, kept):
    size = away.shape[0] // 4
    width = away.shape[1]
    got = swap(away, 1)
    own, *pieces = run(
        pile_core_kernel, [shape((size, width))] + [shape((size, width), BF)] * 3, [kept, got]
    )
    got = [swap(pieces[k - 1], 2 * k) for k in range(1, 4)]
    if short_line():
        (shard,) = run(pile_sum_kernel, [shape((size, width), BF)], [own, *got])
        got = [pass_line(shard, k) for k in range(1, 4)]
        (shard,) = run(pile_sum_kernel, [shape((size, width), BF)], [shard, *got])
    else:
        (shard,) = run(pile_sum_kernel, [shape((size, width))], [own, *got])
        shard = lax.psum(shard, "z").astype(BF)
    pieces = [shard] + [swap(shard, 2 * k) for k in range(1, 4)]
    return pieces + [swap(piece, 1) for piece in pieces]


def first_sum_kernel(near_ref, far_ref, *refs):
    refs, out_ref = refs[:8], refs[8]
    count, rows, width = refs[0].shape
    total = jnp.zeros((rows, width), F32)
    for n, ref in enumerate(refs):
        adjacent_ref = far_ref if n >= 4 else near_ref
        at = n % 4 * count * rows
        total = total + dot(
            adjacent_ref[:, at : at + count * rows], ref[...].reshape(count * rows, width)
        )
    centre_into(out_ref, total)


def per_device(
    features,
    adjacency,
    tile_mask,
    labels,
    train_mask,
    w_first,
    w_second,
    w_head,
    norm_params,
    head_bias,
    m_first,
    m_second,
    m_head,
    m_norms,
    m_bias,
    v_first,
    v_second,
    v_head,
    v_norms,
    v_bias,
):
    rows, node_total = adjacency.shape
    inputs, hidden = w_first.shape
    classes = w_head.shape[1]
    half = node_total // 2
    length = lax.axis_size("z")
    tall = rows + EXTRA
    inputs_tall = -(-inputs // EXTRA) * EXTRA
    head_turned = w_head.T
    work = 2 * rows * node_total * hidden

    if short_line():
        level_shapes = [shape((rows, 8 * rows), BF)] * 4
    else:
        level_shapes = [shape((length, rows, 8 * rows), BF)]
    near, far, notes, *levels = run(
        arrange_kernel,
        [shape((rows, half), BF)] * 2 + [shape((8, LANES))] + level_shapes,
        [tile_mask, adjacency, labels[None], train_mask[None], head_bias[None]],
        scalars=1,
    )

    projected = dot(features, w_first.astype(BF)).astype(BF)
    turned = features.T
    turned = jnp.stack([turned] + [swap(turned, 2 * k) for k in range(1, 4)])
    short = short_line()
    if not short:
        levels = [lax.all_to_all(levels[0], "z", 0, 0)]
    around, passed, unused = gather_all(
        projected, [(levels[1], 1), (levels[2], 2)] if short else ()
    )
    if short:
        levels[1:3] = passed
    (summed_one,) = run(
        first_sum_kernel, [shape((tall, hidden), BF)], [near, far, *around], flops=work
    )
    around, passed, unused = gather_all(summed_one, [(levels[3], 3)] if short else ())
    if short:
        levels[3:] = passed
    summed_two, stats_one = run(
        functools.partial(layer_kernel, node_total, 0),
        [shape((tall, hidden), BF), shape((8, hidden))],
        [near, far, w_second, norm_params, *around],
        flops=3 * work,
    )
    (slopes_one,) = run(
        functools.partial(slopes_kernel, 0),
        [shape((rows, 2 * hidden))],
        [near, far, norm_params, stats_one, *around],
        flops=3 * work,
    )
    if short:
        mixed_shapes = [shape((inputs, rows))] + [shape((inputs, rows), BF)] * 3
    else:
        mixed_shapes = [shape((length, inputs, rows))]
    mixed = run(
        mix_kernel, mixed_shapes, [turned, swap(turned, 1), *levels], flops=2 * work
    )
    around, passed, (slopes_one,) = gather_all(
        summed_two, [(mixed[k], k) for k in (3, 2, 1)] if short else (), [slopes_one]
    )
    if short:
        mixed = [mixed[0], *passed[::-1]]
    else:
        mixed = [lax.psum_scatter(mixed[0], "z", scatter_dimension=0)]
    packed, stats_two = run(
        functools.partial(head_kernel, node_total),
        [shape((HEAD_ROWS + EXTRA, rows), BF), shape((8, hidden))],
        [
            near,
            far,
            head_turned,
            norm_params,
            notes,
            *around,
        ],
        scratch=[
            pltpu.VMEM((rows, LANES + 2 * hidden), F32),
            pltpu.VMEM((8, LANES), F32),
            pltpu.VMEM((LANES, hidden), F32),
        ],
        flops=4 * work,
    )

    packed, head_grad, sums_two = run(
        functools.partial(second_kernel, node_total),
        [shape((hidden + EXTRA, rows), BF), shape((HEAD_ROWS, hidden)), shape((8, LANES))],
        [
            head_turned,
            w_second,
            norm_params,
            summed_two,
            stats_two,
            slopes_one,
            *spread_back(packed, levels, HEAD_ROWS),
        ],
        scratch=[pltpu.VMEM((8, LANES), F32), pltpu.VMEM((LANES, hidden), F32)],
        flops=work // 4,
    )
    size = -(-(inputs_tall + hidden + HEAD_ROWS) // (8 * EXTRA)) * EXTRA
    away, kept, sums_one = run(
        functools.partial(first_kernel, node_total, inputs_tall, len(mixed)),
        [shape((4 * size, hidden), BF), shape((4 * size, hidden)), shape((8, LANES))],
        [
            w_second,
            norm_params,
            summed_one,
            stats_one,
            head_grad,
            *mixed,
            *spread_back(packed, levels, hidden),
        ],
        scratch=[pltpu.VMEM((8 * size, hidden), F32)],
        flops=work,
    )
    matrices = (
        *(w_first, m_first, v_first, w_second, m_second, v_second),
        *(head_turned, m_head.T, v_head.T),
    )
    updated = run(
        functools.partial(update_kernel, inputs_tall),
        [shape(block.shape) for block in matrices],
        [*sum_pile(away, kept), *matrices],
        scratch=[pltpu.VMEM((8 * size, hidden), F32)],
    )
    updated = [*updated[:6], *(block.T for block in updated[6:])]

    def pair(sums):
        return sums[2:4].reshape(1, hidden), sums[0:2].reshape(1, hidden)

    norm_grad = jnp.concatenate([*pair(sums_one), *pair(sums_two)])
    norms = adamw(norm_params, norm_grad, m_norms, v_norms, RATE_SMALL)
    bias = adamw(head_bias, sums_two[4, :classes], m_bias, v_bias, RATE_SMALL)
    loss_sum, train_count = sums_two[5, 0], sums_two[5, 1]
    return (
        loss_sum,
        train_count,
        *(
            part
            for n in range(3)
            for part in (updated[n], updated[3 + n], updated[6 + n], norms[n], bias[n])
        ),
    )


def solution(mesh):
    wide_mesh = Mesh(mesh.devices.reshape(-1, 2, 2, 2), EVERY)
    split = (P(EVERY, None),) * 3 + (P(EVERY),) * 2
    return jax.shard_map(
        per_device,
        mesh=wide_mesh,
        in_specs=split + (P(),) * 15,
        out_specs=(P(),) * 17,
        check_vma=False,
    )
```

```python
import functools
import math

import jax
import jax.numpy as jnp
from jax import lax
from jax.experimental import pallas as pl
from jax.experimental.pallas import tpu as pltpu
from jax.sharding import Mesh
from jax.sharding import PartitionSpec as P

TILE = 128
STEP = 10
EPS_NORM = 1e-05
EPS_ADAM = 1e-08
BETA_ONE = 0.9
BETA_TWO = 0.999
DECAY = 0.01
RATE_MATRIX = 0.03
RATE_SMALL = 0.3

BF = jnp.bfloat16
F32 = jnp.float32
PLANE = ("y", "x", "c")
EVERY = ("z", "y", "x", "c")
LANES = 128
HEAD_ROWS = 48
EXTRA = 16
ROOT = math.sqrt(2.0 / math.pi)
BEND = 0.044715


def adamw(weight, gradient, first, second, rate):
    first_new = BETA_ONE * first + (1.0 - BETA_ONE) * gradient
    second_new = BETA_TWO * second + (1.0 - BETA_TWO) * gradient * gradient
    scaled = (
        first_new
        / (1.0 - BETA_ONE**STEP)
        / (jnp.sqrt(second_new / (1.0 - BETA_TWO**STEP)) + EPS_ADAM)
    )
    return (weight - rate * (scaled + DECAY * weight), first_new, second_new)


def dot(left, right):
    return jnp.dot(left, right, preferred_element_type=F32)


def dot_turned(left, right):
    return lax.dot_general(left, right, (((1,), (1,)), ((), ())), preferred_element_type=F32)


def shape(dims, kind=F32):
    return jax.ShapeDtypeStruct(dims, kind)


def run(body, outs, ins, scratch=(), flops=0, scalars=0):
    held = sum(math.prod(a.shape[:-1]) * max(a.shape[-1], LANES) * a.dtype.itemsize for a in (*ins, *outs))
    limit = min(60 << 20, 2 * held + (8 << 20))
    return pl.pallas_call(
        body,
        out_shape=tuple(outs),
        in_specs=[pl.BlockSpec(memory_space=pltpu.SMEM)] * scalars
        + [pl.BlockSpec(memory_space=pltpu.VMEM)] * (len(ins) - scalars),
        out_specs=tuple(pl.BlockSpec(memory_space=pltpu.VMEM) for unused in outs),
        scratch_shapes=list(scratch),
        compiler_params=pltpu.CompilerParams(vmem_limit_bytes=limit),
        cost_estimate=pl.CostEstimate(flops=flops, bytes_accessed=held, transcendentals=0),
    )(*ins)


def swap(block, mask):
    return lax.ppermute(block, PLANE, [(i, i ^ mask) for i in range(8)])


def pass_line(block, mask):
    return lax.ppermute(block, "z", [(i, i ^ mask) for i in range(4)])


def short_line():
    return lax.axis_size("z") == 4


def after(block, *others):
    return lax.optimization_barrier((block, *others))[0]


def stack_kernel(*refs):
    refs, out_ref = refs[3::-1], refs[4]
    for k, ref in enumerate(refs):
        out_ref[k] = ref[...]


def line_kernel(*refs):
    refs, (out_ref, centres_ref) = refs[3::-1], refs[4:]
    rows = refs[0].shape[0] - EXTRA
    centres_ref[...] = jnp.zeros(centres_ref.shape, F32)
    for k, ref in enumerate(refs):
        out_ref[k * rows : (k + 1) * rows, :] = ref[:rows, :]
        centres_ref[k : k + 1, :] = ref[rows:, :].astype(F32)[:1]
    out_ref[4 * rows :, :] = centres_ref[...].astype(BF)


def gather_all(block, beside=(), within=(), centred=True, early=()):
    if short_line():
        line = [block] + [pass_line(block, k) for k in range(1, 4)]
        if centred:
            tall, width = block.shape
            (line,) = run(
                line_kernel,
                [shape((4 * tall - 3 * EXTRA, width), BF)],
                line[::-1],
                scratch=[pltpu.VMEM((EXTRA, width), F32)],
            )
        else:
            (line,) = run(stack_kernel, [shape((4, *block.shape), BF)], line[::-1])
    else:
        line = lax.all_gather(block, "z", axis=0)
    if early:
        line, *early = lax.optimization_barrier((line, *early))
    passed = [pass_line(after(part, line), mask) for part, mask in beside]
    lines = [line] + [swap(line, 2 * k) for k in range(1, 4)]
    if passed or within:
        lines[3], *rest = lax.optimization_barrier((lines[3], *passed, *within))
        passed, within = rest[: len(passed)], rest[len(passed) :]
    return lines + [swap(line, 1) for line in lines], passed, within, early


def arrange_kernel(
    mask_ref, values_ref, label_ref, train_ref, bias_ref, near_ref, far_ref, notes_ref, *level_refs
):
    notes_ref[...] = jnp.zeros(notes_ref.shape, F32)
    notes_ref[0:1, :] = label_ref[...].astype(F32)
    notes_ref[1:2, :] = train_ref[...].astype(F32)
    notes_ref[2:3, : bias_ref.shape[1]] = bias_ref[...]
    half = near_ref.shape[1] // TILE
    lines = half // 4
    here = 4 * lax.axis_index("y") + 2 * lax.axis_index("x") + lax.axis_index("c")
    level = lax.axis_index("z") if short_line() else 0

    for core, out_ref in ((0, near_ref), (1, far_ref)):
        for place in range(4):

            def one(step, carry, core=core, place=place, out_ref=out_ref):
                source = jnp.bitwise_xor(step, level) * 8 + jnp.bitwise_xor(place * 2 + core, here)
                keep = mask_ref[0, source].astype(F32).astype(BF)
                block = values_ref[:, pl.ds(pl.multiple_of(source * TILE, TILE), TILE)] * keep
                at = pl.multiple_of((place * lines + step) * TILE, TILE)
                out_ref[:, pl.ds(at, TILE)] = block
                cols = slice((core * 4 + place) * TILE, (core * 4 + place + 1) * TILE)
                if len(level_refs) == 1:
                    level_refs[0][step, :, cols] = block
                else:
                    level_refs[step][:, cols] = block
                return carry

            if len(level_refs) == 1:
                lax.fori_loop(0, lines, one, 0)
            else:
                for step in range(lines):
                    one(step, 0)


def centre_into(out_ref, summed):
    rows = summed.shape[0]
    centre = (jnp.sum(summed, axis=0, keepdims=True) / rows).astype(BF).astype(F32)
    out_ref[:rows, :] = (summed - centre).astype(BF)
    out_ref[rows:, :] = jnp.broadcast_to(centre, (EXTRA, summed.shape[1])).astype(BF)


def block_at(ref, i, rows):
    if len(ref.shape) == 3:
        return ref[i, :rows, :].astype(F32), ref[i, rows:, :].astype(F32)[:1]
    return (
        ref[i * rows : (i + 1) * rows, :].astype(F32),
        ref[4 * rows :, :].astype(F32)[i : i + 1],
    )


def block_loop(ref, pair, body, carry):
    if len(ref.shape) == 3:
        return lax.fori_loop(
            0, ref.shape[0] // pair, lambda i, carry: body(i * pair, carry), carry
        )
    for i in range(0, 4, pair):
        carry = body(i, carry)
    return carry


def moments(refs, rows, node_total):
    width = refs[0].shape[-1]
    pivot = block_at(refs[0], 0, rows)[1]
    zero = jnp.zeros((8, width), F32)
    sums = (zero, zero)
    for ref in refs:

        def one(i, carry, ref=ref):
            total, square = carry
            value, centre = block_at(ref, i, rows)
            value = value.reshape(rows // 8, 8, width)
            part = jnp.sum(value, axis=0)
            away = centre - pivot
            each = away * (rows // 8)
            return (
                total + part + each,
                square + jnp.sum(value * value, axis=0) + away * (2.0 * part + each),
            )

        sums = block_loop(ref, 1, one, sums)
    shift = jnp.sum(sums[0], axis=0, keepdims=True) / node_total
    variance = jnp.sum(sums[1], axis=0, keepdims=True) / node_total - shift * shift
    return pivot + shift, lax.rsqrt(jnp.maximum(variance, 0.0) + EPS_NORM)


def gelu_half(value):
    square = value * value
    bend = jnp.tanh(value * (ROOT + (ROOT * BEND) * square))
    return 0.5 + 0.5 * bend, square


def gelu_slope(value, half, square):
    return half + (value * half) * (1.0 - half) * (2 * ROOT + (6 * ROOT * BEND) * square)


def with_columns(refs, near_ref, far_ref, act, total):
    rows, columns = near_ref.shape
    for n, ref in enumerate(refs):
        adjacent_ref = far_ref if n >= 4 else near_ref

        def one(i, total, ref=ref, adjacent_ref=adjacent_ref, at=n % 4 * (columns // 4)):
            start = at + i * rows
            if not isinstance(start, int):
                start = pl.multiple_of(start, 4 * rows)
            blocks = [block_at(ref, i + j, rows) for j in range(4)]
            return act(blocks, adjacent_ref[:, pl.ds(start, 4 * rows)], total)

        total = block_loop(ref, 4, one, total)
    return total


def split_sums(total):
    high = total.astype(BF).astype(F32)
    low = (total - high).astype(BF).astype(F32)
    return jnp.concatenate([high, low])


def joined(parts):
    parts = parts.astype(F32)
    return parts[: EXTRA // 2] + parts[EXTRA // 2 :]


def put_sums(out_ref, width, parts):
    out_ref[width:, :LANES] = parts.astype(BF)
    if out_ref.shape[1] > LANES:
        out_ref[width:, LANES:] = jnp.zeros((EXTRA, out_ref.shape[1] - LANES), BF)


def pack_into(out_ref, turned, parts):
    width = turned.shape[0]
    out_ref[:width, :] = turned.astype(BF)
    if parts is not None:
        put_sums(out_ref, width, parts)


def add_up(values):
    values = list(values)
    while len(values) > 1:
        values = [values[i] + values[i + 1] for i in range(0, len(values), 2)]
    return values[0]


def cross(turned_refs, level_refs, start, stop, width, out):
    if len(level_refs) == 1:
        count = level_refs[0].shape[0]
        turned = [turned_refs[0].at[i] for i in range(count)]
        levels = [level_refs[0].at[i] for i in range(count)]
    else:
        turned, levels = turned_refs, level_refs
    total = None
    for i in range(0, len(levels), 2):
        left = jnp.concatenate([turned[i][:width, :], turned[i + 1][:width, :]], axis=1)
        right = jnp.concatenate([levels[i][:, start:stop], levels[i + 1][:, start:stop]])
        part = dot(left, right)
        total = part if total is None else total + part
    out(total)


def cross_kernel(width, count, *refs):
    turned_refs, level_refs, (send_ref,) = refs[:count][::-1], refs[count : 2 * count], refs[2 * count :]
    half = send_ref.shape[1]

    def out(value):
        send_ref[:width, :] = value.astype(BF)

    cross(turned_refs, level_refs, half, 2 * half, width, out)
    if send_ref.shape[0] > width:
        if count == 1:
            parts = [joined(turned_refs[0][i, width:, :]) for i in range(turned_refs[0].shape[0])]
        else:
            parts = [joined(ref[width:, :]) for ref in turned_refs]
        put_sums(send_ref, width, split_sums(add_up(parts)))


def keep_kernel(width, count, *refs):
    turned_refs, level_refs, (out_ref,) = refs[:count][::-1], refs[count : 2 * count], refs[2 * count :]

    def out(value):
        out_ref[...] = value

    cross(turned_refs, level_refs, 0, out_ref.shape[1], width, out)


def fold_kernel(kept_ref, send_ref, got_ref, own_ref, *piece_refs):
    width = kept_ref.shape[0]
    for k in range(4):
        cols = slice(k * LANES, (k + 1) * LANES)
        value = kept_ref[:, cols] + got_ref[:width, cols].astype(F32)
        if k == 0:
            own_ref[:width, :] = value
        else:
            piece_refs[k - 1][:width, :] = value.astype(BF)
    if own_ref.shape[0] > width:
        parts = split_sums(joined(send_ref[width:, :LANES]) + joined(got_ref[width:, :LANES]))
        own_ref[width:, :] = parts
        for piece_ref in piece_refs:
            put_sums(piece_ref, width, parts)


def spread_back(packed, levels, width):
    tall = packed.shape[0]
    if short_line():
        turned = [packed] + [pass_line(packed, k) for k in range(1, 4)]
    else:
        turned = [lax.all_gather(packed, "z", axis=0)]
    count = len(levels)
    half = levels[0].shape[-1] // 2
    work = 8 * width * LANES * half
    (send,) = run(
        functools.partial(cross_kernel, width, count),
        [shape((tall, half), BF)],
        [*turned[::-1], *levels],
        flops=work,
    )
    got = swap(send, 1)
    (kept,) = run(
        functools.partial(keep_kernel, width, count),
        [shape((width, half))],
        [*turned[::-1], *levels],
        flops=work,
    )
    own, *pieces = run(
        fold_kernel, [shape((tall, LANES))] + [shape((tall, LANES), BF)] * 3, [kept, send, got]
    )
    return [swap(pieces[k - 1], 2 * k) for k in (3, 2, 1)] + [own]


def line_total(refs, width):
    total = add_up(ref[:width, :].astype(F32) for ref in refs)
    if refs[0].shape[0] == width:
        return total, None
    return total, add_up(joined(ref[width:, :]) for ref in refs)


def wide(sums, row):
    return jnp.concatenate([sums[row : row + 1], sums[row + 1 : row + 2]], axis=1)


def put_wide(ref, row, value):
    ref[row : row + 1, :] = value[:, :LANES]
    ref[row + 1 : row + 2, :] = value[:, LANES:]


def layer_kernel(node_total, layer, near_ref, far_ref, weight_ref, norm_ref, *refs):
    refs, (out_ref, stats_ref) = refs[:8], refs[8:]
    rows, width = near_ref.shape[0], refs[0].shape[-1]
    mean_value, inverse = moments(refs, rows, node_total)
    stats_ref[0:1, :] = mean_value
    stats_ref[1:2, :] = inverse
    scale = norm_ref[2 * layer : 2 * layer + 1, :] * inverse
    start = norm_ref[2 * layer + 1 : 2 * layer + 2, :] - mean_value * scale
    low = weight_ref[...].astype(BF)

    def act(blocks, adjacent, total):
        hidden = []
        for value, centre in blocks:
            value = value * scale + (start + centre * scale)
            hidden.append((value * gelu_half(value)[0]).astype(BF))
        projected = dot(jnp.concatenate(hidden), low).astype(BF)
        return total + dot(adjacent, projected)

    total = jnp.zeros((rows, low.shape[1]), F32)
    centre_into(out_ref, with_columns(refs, near_ref, far_ref, act, total))


def slopes_kernel(layer, near_ref, far_ref, norm_ref, stats_ref, *refs):
    refs, out_ref = refs[:8], refs[8]
    mean_value, inverse = stats_ref[0:1, :], stats_ref[1:2, :]
    gain = norm_ref[2 * layer : 2 * layer + 1, :]
    offset = norm_ref[2 * layer + 1 : 2 * layer + 2, :]
    out_ref[...] = jnp.zeros(out_ref.shape, F32)

    def act(blocks, adjacent, carry):
        slopes = []
        for value, centre in blocks:
            normed = value * inverse + (centre - mean_value) * inverse
            value = gain * normed + offset
            slope = gelu_slope(value, *gelu_half(value))
            slopes.append(jnp.concatenate([slope.astype(BF), (slope * normed).astype(BF)], axis=1))
        out_ref[...] += dot(adjacent, jnp.concatenate(slopes))
        return carry

    with_columns(refs, near_ref, far_ref, act, 0)


def head_low_of(weight_ref, tall_ref):
    tall_ref[...] = jnp.zeros(tall_ref.shape, F32)
    tall_ref[: weight_ref.shape[0], :] = weight_ref[...]
    return tall_ref[...].astype(BF)


def head_kernel(node_total, near_ref, far_ref, weight_ref, norm_ref, notes_ref, *refs):
    refs, (packed_ref, stats_ref, total_ref, sums_ref, tall_ref) = refs[:8], refs[8:]
    rows, width = near_ref.shape[0], refs[0].shape[-1]
    classes = weight_ref.shape[0]
    mean_value, inverse = moments(refs, rows, node_total)
    stats_ref[0:1, :] = mean_value
    stats_ref[1:2, :] = inverse
    gain, offset = norm_ref[2:3, :], norm_ref[3:4, :]
    low = head_low_of(weight_ref, tall_ref)
    total_ref[...] = jnp.zeros(total_ref.shape, F32)

    def act(blocks, adjacent, carry):
        hidden, slopes = [], []
        for value, centre in blocks:
            normed = value * inverse + (centre - mean_value) * inverse
            value = gain * normed + offset
            half, square = gelu_half(value)
            slope = gelu_slope(value, half, square)
            hidden.append((value * half).astype(BF))
            slopes.append(jnp.concatenate([slope.astype(BF), (slope * normed).astype(BF)], axis=1))
        headed = dot_turned(jnp.concatenate(hidden), low).astype(BF)
        both = jnp.concatenate([headed, jnp.concatenate(slopes)], axis=1)
        total_ref[...] += dot(adjacent, both)
        return carry

    with_columns(refs, near_ref, far_ref, act, 0)

    lane = lax.broadcasted_iota(jnp.int32, (rows, LANES), 1)
    sums_ref[...] = jnp.zeros(sums_ref.shape, F32)
    logits = jnp.where(lane < classes, total_ref[:, :LANES] + notes_ref[2:3, :], -1e30)
    logits = logits - jnp.max(logits, axis=1, keepdims=True)
    raised = jnp.exp(logits)
    whole = jnp.sum(raised, axis=1, keepdims=True)
    label = jnp.broadcast_to(notes_ref[0:1, :], (LANES, rows)).T
    onehot = jnp.where(lane.astype(F32) == label, 1.0, 0.0)
    weight = jnp.broadcast_to(notes_ref[1:2, :], (LANES, rows)).T
    losses = jnp.log(whole) - jnp.sum(onehot * logits, axis=1, keepdims=True)
    d_logits = (raised / whole - onehot) * weight
    d_low = d_logits.astype(BF)
    d_wide = dot(d_low, low)
    put_wide(sums_ref, 0, jnp.sum(d_wide * total_ref[:, LANES : LANES + width], axis=0, keepdims=True))
    put_wide(sums_ref, 2, jnp.sum(d_wide * total_ref[:, LANES + width :], axis=0, keepdims=True))
    sums_ref[4:5, :] = jnp.sum(d_logits, axis=0, keepdims=True)
    sums_ref[5:6, :] = jnp.sum(
        jnp.where(lane == 0, losses * weight, weight), axis=0, keepdims=True
    )
    pack_into(packed_ref, d_logits.T[:HEAD_ROWS], split_sums(sums_ref[...]))


def backward_norm(d_hidden, own_ref, stats_ref, norm_ref, layer, shift_grad, gain_grad, node_total):
    rows = own_ref.shape[0] - EXTRA
    mean_value, inverse = stats_ref[0:1, :], stats_ref[1:2, :]
    gain = norm_ref[2 * layer : 2 * layer + 1, :]
    centre = own_ref[rows:, :].astype(F32)[:1]
    normed = own_ref[:rows, :].astype(F32) * inverse + (centre - mean_value) * inverse
    value = gain * normed + norm_ref[2 * layer + 1 : 2 * layer + 2, :]
    half, square = gelu_half(value)
    d_pre = d_hidden * gelu_slope(value, half, square)
    d_summed = (gain * inverse) * (d_pre - (shift_grad + normed * gain_grad) / node_total)
    return d_summed, value * half


def second_kernel(
    node_total,
    head_ref,
    weight_ref,
    norm_ref,
    summed_ref,
    stats_ref,
    slopes_ref,
    *refs,
):
    refs, (packed_ref, grad_ref, out_ref, sums_ref, tall_ref) = refs[:4], refs[4:]
    headed, sums = line_total(refs, HEAD_ROWS)
    rows = headed.shape[1]
    each = 1.0 / sums[5:6, 1:2]
    headed = headed * each
    put_row = lax.broadcasted_iota(jnp.int32, sums.shape, 0)
    out_ref[...] = jnp.where(put_row == 5, sums, sums * each)
    turned_back = jnp.concatenate([headed, jnp.zeros((LANES - HEAD_ROWS, rows), F32)]).T
    d_hidden = dot(turned_back.astype(BF), head_low_of(head_ref, tall_ref))
    d_summed, hidden = backward_norm(
        d_hidden, summed_ref, stats_ref, norm_ref, 1, wide(sums, 0) * each, wide(sums, 2) * each, node_total
    )
    grad_ref[...] = dot(headed.astype(BF), hidden.astype(BF))
    d_wide = dot_turned(d_summed.astype(BF), weight_ref[...].astype(BF))
    width = d_wide.shape[1]
    put_wide(sums_ref, 0, jnp.sum(d_wide * slopes_ref[:, :width], axis=0, keepdims=True))
    put_wide(sums_ref, 2, jnp.sum(d_wide * slopes_ref[:, width:], axis=0, keepdims=True))
    sums_ref[4:8, :] = jnp.zeros((4, LANES), F32)
    pack_into(packed_ref, d_summed.T, split_sums(sums_ref[...]))


def mix_kernel(near_ref, far_ref, *refs):
    outs = 1 if len(refs) == 2 else 4
    level_refs, out_refs = refs[:outs], refs[outs:]

    def one(level_ref):
        total = None
        for n in range(0, 8, 2):
            ref = far_ref if n >= 4 else near_ref
            left = jnp.concatenate([ref[n % 4], ref[n % 4 + 1]], axis=1)
            part = dot_turned(left, level_ref[:, n * TILE : (n + 2) * TILE])
            total = part if total is None else total + part
        return total

    if outs == 1:

        def step(i, carry):
            out_refs[0][i] = one(level_refs[0].at[i])
            return carry

        lax.fori_loop(0, level_refs[0].shape[0], step, 0)
        return
    for level_ref, out_ref in zip(level_refs, out_refs, strict=True):
        out_ref[...] = one(level_ref).astype(out_ref.dtype)


def first_kernel(node_total, inputs_tall, mixes, weight_ref, norm_ref, summed_ref, stats_ref, head_ref, *refs):
    mix_refs, refs = refs[:mixes], refs[mixes:]
    refs, (away_ref, kept_ref, out_ref, pile_ref) = refs[:4], refs[4:]
    width = weight_ref.shape[1]
    d_projected, sums = line_total(refs, width)
    out_ref[...] = sums
    d_projected = d_projected.T.astype(BF)
    d_hidden = dot_turned(d_projected, weight_ref[...].astype(BF))
    d_summed, hidden = backward_norm(
        d_hidden, summed_ref, stats_ref, norm_ref, 0, wide(sums, 0), wide(sums, 2), node_total
    )
    mixed = add_up(ref[...].astype(F32) for ref in mix_refs).astype(BF)
    pile_ref[...] = jnp.zeros(pile_ref.shape, F32)
    pile_ref[: mixed.shape[0], :] = dot(mixed, d_summed.astype(BF))
    at = inputs_tall
    pile_ref[at : at + width, :] = dot(hidden.T.astype(BF), d_projected)
    at += width
    pile_ref[at : at + HEAD_ROWS, :] = head_ref[...]
    half = away_ref.shape[0]
    core = lax.axis_index("c")
    away_ref[...] = pile_ref[pl.ds(pl.multiple_of((1 - core) * half, half), half), :].astype(BF)
    kept_ref[...] = pile_ref[pl.ds(pl.multiple_of(core * half, half), half), :]


def pile_core_kernel(kept_ref, got_ref, own_ref, *piece_refs):
    size = own_ref.shape[0]
    here = 2 * lax.axis_index("y") + lax.axis_index("x")
    for k in range(4):
        at = pl.ds(pl.multiple_of(jnp.bitwise_xor(here, k) * size, size), size)
        value = kept_ref[at, :] + got_ref[at, :].astype(F32)
        if k == 0:
            own_ref[...] = value
        else:
            piece_refs[k - 1][...] = value.astype(BF)


def pile_sum_kernel(own_ref, *refs):
    parts = [own_ref, *refs[:3]]
    refs[3][...] = add_up(ref[...].astype(F32) for ref in parts).astype(refs[3].dtype)


def update_kernel(inputs_tall, *refs):
    pieces, refs = refs[:8], refs[8:]
    inputs, outs, pile_ref = refs[:9], refs[9:18], refs[18]
    size, width = pieces[0].shape
    here = 2 * lax.axis_index("y") + lax.axis_index("x")
    core = lax.axis_index("c")
    for n, ref in enumerate(pieces):
        at = (jnp.bitwise_xor(core, n // 4) * 4 + jnp.bitwise_xor(here, n % 4)) * size
        pile_ref[pl.ds(pl.multiple_of(at, size), size), :] = ref[...].astype(F32)
    tall = inputs[0].shape[0]
    grads = (
        pile_ref[:tall, :],
        pile_ref[inputs_tall : inputs_tall + width, :],
        pile_ref[inputs_tall + width : inputs_tall + width + inputs[6].shape[0], :],
    )
    for n in range(3):
        weight, first, second = (ref[...] for ref in inputs[3 * n : 3 * n + 3])
        results = adamw(weight, grads[n], first, second, RATE_MATRIX)
        for ref, value in zip(outs[3 * n : 3 * n + 3], results, strict=True):
            ref[...] = value


def sum_pile(away, kept):
    size = away.shape[0] // 4
    width = away.shape[1]
    got = swap(away, 1)
    own, *pieces = run(
        pile_core_kernel, [shape((size, width))] + [shape((size, width), BF)] * 3, [kept, got]
    )
    got = [swap(pieces[k - 1], 2 * k) for k in range(1, 4)]
    if short_line():
        (shard,) = run(pile_sum_kernel, [shape((size, width), BF)], [own, *got])
        got = [pass_line(shard, k) for k in range(1, 4)]
        (shard,) = run(pile_sum_kernel, [shape((size, width), BF)], [*got[::-1], shard])
    else:
        (shard,) = run(pile_sum_kernel, [shape((size, width))], [own, *got])
        shard = lax.psum(shard, "z").astype(BF)
    pieces = [shard] + [swap(shard, 2 * k) for k in range(1, 4)]
    return pieces + [swap(piece, 1) for piece in pieces]


def first_sum_kernel(near_ref, far_ref, *refs):
    refs, out_ref = refs[:8], refs[8]
    count, rows, width = refs[0].shape
    total = jnp.zeros((rows, width), F32)
    for n, ref in enumerate(refs):
        adjacent_ref = far_ref if n >= 4 else near_ref
        at = n % 4 * count * rows
        total = total + dot(
            adjacent_ref[:, at : at + count * rows], ref[...].reshape(count * rows, width)
        )
    centre_into(out_ref, total)


def per_device(
    features,
    adjacency,
    tile_mask,
    labels,
    train_mask,
    w_first,
    w_second,
    w_head,
    norm_params,
    head_bias,
    m_first,
    m_second,
    m_head,
    m_norms,
    m_bias,
    v_first,
    v_second,
    v_head,
    v_norms,
    v_bias,
):
    rows, node_total = adjacency.shape
    inputs, hidden = w_first.shape
    classes = w_head.shape[1]
    half = node_total // 2
    length = lax.axis_size("z")
    tall = rows + EXTRA
    inputs_tall = -(-inputs // EXTRA) * EXTRA
    head_turned = w_head.T
    work = 2 * rows * node_total * hidden

    if short_line():
        level_shapes = [shape((rows, 8 * rows), BF)] * 4
    else:
        level_shapes = [shape((length, rows, 8 * rows), BF)]
    near, far, notes, *levels = run(
        arrange_kernel,
        [shape((rows, half), BF)] * 2 + [shape((8, LANES))] + level_shapes,
        [tile_mask, adjacency, labels[None], train_mask[None], head_bias[None]],
        scalars=1,
    )

    projected = dot(features, w_first.astype(BF)).astype(BF)
    turned = features.T
    short = short_line()
    if not short:
        levels = [lax.all_to_all(levels[0], "z", 0, 0)]
    around, passed, unused, (turned_x,) = gather_all(
        projected,
        [(levels[1], 1), (levels[2], 2)] if short else (),
        centred=False,
        early=[swap(turned, 2)],
    )
    turned = jnp.stack([turned, turned_x])
    turned = jnp.concatenate([turned, swap(turned, 4)])
    if short:
        levels[1:3] = passed
    (summed_one,) = run(
        first_sum_kernel, [shape((tall, hidden), BF)], [near, far, *around], flops=work
    )
    around, passed, *unused = gather_all(summed_one, [(levels[3], 3)] if short else ())
    if short:
        levels[3:] = passed
    summed_two, stats_one = run(
        functools.partial(layer_kernel, node_total, 0),
        [shape((tall, hidden), BF), shape((8, hidden))],
        [near, far, w_second, norm_params, *around],
        flops=3 * work,
    )
    (slopes_one,) = run(
        functools.partial(slopes_kernel, 0),
        [shape((rows, 2 * hidden))],
        [near, far, norm_params, stats_one, *around],
        flops=3 * work,
    )
    if short:
        mixed_shapes = [shape((inputs, rows))] + [shape((inputs, rows), BF)] * 3
    else:
        mixed_shapes = [shape((length, inputs, rows))]
    mixed = run(
        mix_kernel, mixed_shapes, [turned, swap(turned, 1), *levels], flops=2 * work
    )
    around, passed, (slopes_one,), unused = gather_all(
        summed_two, [(mixed[k], k) for k in (1, 2, 3)] if short else (), [slopes_one]
    )
    if short:
        mixed = [mixed[0], *passed]
    else:
        mixed = [lax.psum_scatter(mixed[0], "z", scatter_dimension=0)]
    packed, stats_two = run(
        functools.partial(head_kernel, node_total),
        [shape((HEAD_ROWS + EXTRA, rows), BF), shape((8, hidden))],
        [
            near,
            far,
            head_turned,
            norm_params,
            notes,
            *around,
        ],
        scratch=[
            pltpu.VMEM((rows, LANES + 2 * hidden), F32),
            pltpu.VMEM((8, LANES), F32),
            pltpu.VMEM((LANES, hidden), F32),
        ],
        flops=4 * work,
    )

    packed, head_grad, sums_two = run(
        functools.partial(second_kernel, node_total),
        [shape((hidden + EXTRA, rows), BF), shape((HEAD_ROWS, hidden)), shape((8, LANES))],
        [
            head_turned,
            w_second,
            norm_params,
            summed_two,
            stats_two,
            slopes_one,
            *spread_back(packed, levels, HEAD_ROWS),
        ],
        scratch=[pltpu.VMEM((8, LANES), F32), pltpu.VMEM((LANES, hidden), F32)],
        flops=work // 4,
    )
    size = -(-(inputs_tall + hidden + HEAD_ROWS) // (8 * EXTRA)) * EXTRA
    away, kept, sums_one = run(
        functools.partial(first_kernel, node_total, inputs_tall, len(mixed)),
        [shape((4 * size, hidden), BF), shape((4 * size, hidden)), shape((8, LANES))],
        [
            w_second,
            norm_params,
            summed_one,
            stats_one,
            head_grad,
            *mixed,
            *spread_back(packed, levels, hidden),
        ],
        scratch=[pltpu.VMEM((8 * size, hidden), F32)],
        flops=work,
    )
    matrices = (
        *(w_first, m_first, v_first, w_second, m_second, v_second),
        *(head_turned, m_head.T, v_head.T),
    )
    updated = run(
        functools.partial(update_kernel, inputs_tall),
        [shape(block.shape) for block in matrices],
        [*sum_pile(away, kept), *matrices],
        scratch=[pltpu.VMEM((8 * size, hidden), F32)],
    )
    updated = [*updated[:6], *(block.T for block in updated[6:])]

    def pair(sums):
        return sums[2:4].reshape(1, hidden), sums[0:2].reshape(1, hidden)

    norm_grad = jnp.concatenate([*pair(sums_one), *pair(sums_two)])
    norms = adamw(norm_params, norm_grad, m_norms, v_norms, RATE_SMALL)
    bias = adamw(head_bias, sums_two[4, :classes], m_bias, v_bias, RATE_SMALL)
    loss_sum, train_count = sums_two[5, 0], sums_two[5, 1]
    return (
        loss_sum,
        train_count,
        *(
            part
            for n in range(3)
            for part in (updated[n], updated[3 + n], updated[6 + n], norms[n], bias[n])
        ),
    )


def solution(mesh):
    wide_mesh = Mesh(mesh.devices.reshape(-1, 2, 2, 2), EVERY)
    split = (P(EVERY, None),) * 3 + (P(EVERY),) * 2
    return jax.shard_map(
        per_device,
        mesh=wide_mesh,
        in_specs=split + (P(),) * 15,
        out_specs=(P(),) * 17,
        check_vma=False,
    )
```

```python
import functools
import math

import jax
import jax.numpy as jnp
from jax import lax
from jax.experimental import pallas as pl
from jax.experimental.pallas import tpu as pltpu
from jax.sharding import Mesh
from jax.sharding import PartitionSpec as P

TILE = 128
STEP = 10
EPS_NORM = 1e-05
EPS_ADAM = 1e-08
BETA_ONE = 0.9
BETA_TWO = 0.999
DECAY = 0.01
RATE_MATRIX = 0.03
RATE_SMALL = 0.3

BF = jnp.bfloat16
F32 = jnp.float32
PLANE = ("y", "x", "c")
EVERY = ("z", "y", "x", "c")
LANES = 128
HEAD_ROWS = 48
EXTRA = 16
ROOT = math.sqrt(2.0 / math.pi)
BEND = 0.044715


def adamw(weight, gradient, first, second, rate):
    first_new = BETA_ONE * first + (1.0 - BETA_ONE) * gradient
    second_new = BETA_TWO * second + (1.0 - BETA_TWO) * gradient * gradient
    scaled = (
        first_new
        / (1.0 - BETA_ONE**STEP)
        / (jnp.sqrt(second_new / (1.0 - BETA_TWO**STEP)) + EPS_ADAM)
    )
    return (weight - rate * (scaled + DECAY * weight), first_new, second_new)


def dot(left, right):
    return jnp.dot(left, right, preferred_element_type=F32)


def dot_turned(left, right):
    return lax.dot_general(left, right, (((1,), (1,)), ((), ())), preferred_element_type=F32)


def shape(dims, kind=F32):
    return jax.ShapeDtypeStruct(dims, kind)


def run(body, outs, ins, scratch=(), flops=0, scalars=0):
    held = sum(math.prod(a.shape[:-1]) * max(a.shape[-1], LANES) * a.dtype.itemsize for a in (*ins, *outs))
    limit = min(60 << 20, 2 * held + (8 << 20))
    return pl.pallas_call(
        body,
        out_shape=tuple(outs),
        in_specs=[pl.BlockSpec(memory_space=pltpu.SMEM)] * scalars
        + [pl.BlockSpec(memory_space=pltpu.VMEM)] * (len(ins) - scalars),
        out_specs=tuple(pl.BlockSpec(memory_space=pltpu.VMEM) for unused in outs),
        scratch_shapes=list(scratch),
        compiler_params=pltpu.CompilerParams(vmem_limit_bytes=limit),
        cost_estimate=pl.CostEstimate(flops=flops, bytes_accessed=held, transcendentals=0),
    )(*ins)


def swap(block, mask):
    return lax.ppermute(block, PLANE, [(i, i ^ mask) for i in range(8)])


def pass_line(block, mask):
    return lax.ppermute(block, "z", [(i, i ^ mask) for i in range(4)])


def short_line():
    return lax.axis_size("z") == 4


def after(block, *others):
    return lax.optimization_barrier((block, *others))[0]


def stack_kernel(*refs):
    refs, out_ref = refs[3::-1], refs[4]
    for k, ref in enumerate(refs):
        out_ref[k] = ref[...]


def line_kernel(*refs):
    refs, (out_ref, centres_ref) = refs[3::-1], refs[4:]
    rows = refs[0].shape[0] - EXTRA
    centres_ref[...] = jnp.zeros(centres_ref.shape, F32)
    for k, ref in enumerate(refs):
        out_ref[k * rows : (k + 1) * rows, :] = ref[:rows, :]
        centres_ref[k : k + 1, :] = ref[rows:, :].astype(F32)[:1]
    out_ref[4 * rows :, :] = centres_ref[...].astype(BF)


def gather_all(block, beside=(), within=(), centred=True, early=(), tied=True):
    if short_line():
        line = [block] + [pass_line(block, k) for k in range(1, 4)]
        if centred:
            tall, width = block.shape
            (line,) = run(
                line_kernel,
                [shape((4 * tall - 3 * EXTRA, width), BF)],
                line[::-1],
                scratch=[pltpu.VMEM((EXTRA, width), F32)],
            )
        else:
            (line,) = run(stack_kernel, [shape((4, *block.shape), BF)], line[::-1])
    else:
        line = lax.all_gather(block, "z", axis=0)
    if early:
        line, *early = lax.optimization_barrier((line, *early))
    passed = [pass_line(after(part, line) if tied else part, mask) for part, mask in beside]
    lines = [line] + [swap(line, 2 * k) for k in range(1, 4)]
    if passed or within:
        lines[3], *rest = lax.optimization_barrier((lines[3], *passed, *within))
        passed, within = rest[: len(passed)], rest[len(passed) :]
    return lines + [swap(line, 1) for line in lines], passed, within, early


def arrange_kernel(
    mask_ref, values_ref, label_ref, train_ref, bias_ref, near_ref, far_ref, notes_ref, *level_refs
):
    notes_ref[...] = jnp.zeros(notes_ref.shape, F32)
    notes_ref[0:1, :] = label_ref[...].astype(F32)
    notes_ref[1:2, :] = train_ref[...].astype(F32)
    notes_ref[2:3, : bias_ref.shape[1]] = bias_ref[...]
    half = near_ref.shape[1] // TILE
    lines = half // 4
    here = 4 * lax.axis_index("y") + 2 * lax.axis_index("x") + lax.axis_index("c")
    level = lax.axis_index("z") if short_line() else 0

    for core, out_ref in ((0, near_ref), (1, far_ref)):
        for place in range(4):

            def one(step, carry, core=core, place=place, out_ref=out_ref):
                source = jnp.bitwise_xor(step, level) * 8 + jnp.bitwise_xor(place * 2 + core, here)
                keep = mask_ref[0, source].astype(F32).astype(BF)
                block = values_ref[:, pl.ds(pl.multiple_of(source * TILE, TILE), TILE)] * keep
                at = pl.multiple_of((place * lines + step) * TILE, TILE)
                out_ref[:, pl.ds(at, TILE)] = block
                cols = slice((core * 4 + place) * TILE, (core * 4 + place + 1) * TILE)
                if len(level_refs) == 1:
                    level_refs[0][step, :, cols] = block
                else:
                    level_refs[step][:, cols] = block
                return carry

            if len(level_refs) == 1:
                lax.fori_loop(0, lines, one, 0)
            else:
                for step in range(lines):
                    one(step, 0)


def centre_into(out_ref, summed):
    rows = summed.shape[0]
    centre = (jnp.sum(summed, axis=0, keepdims=True) / rows).astype(BF).astype(F32)
    out_ref[:rows, :] = (summed - centre).astype(BF)
    out_ref[rows:, :] = jnp.broadcast_to(centre, (EXTRA, summed.shape[1])).astype(BF)


def block_at(ref, i, rows):
    if len(ref.shape) == 3:
        return ref[i, :rows, :].astype(F32), ref[i, rows:, :].astype(F32)[:1]
    return (
        ref[i * rows : (i + 1) * rows, :].astype(F32),
        ref[4 * rows :, :].astype(F32)[i : i + 1],
    )


def block_loop(ref, pair, body, carry):
    if len(ref.shape) == 3:
        return lax.fori_loop(
            0, ref.shape[0] // pair, lambda i, carry: body(i * pair, carry), carry
        )
    for i in range(0, 4, pair):
        carry = body(i, carry)
    return carry


def moments_of(refs, rows, pivot, sums):
    width = refs[0].shape[-1]
    for ref in refs:

        def one(i, carry, ref=ref):
            total, square = carry
            value, centre = block_at(ref, i, rows)
            value = value.reshape(rows // 8, 8, width)
            part = jnp.sum(value, axis=0)
            away = centre - pivot
            each = away * (rows // 8)
            return (
                total + part + each,
                square + jnp.sum(value * value, axis=0) + away * (2.0 * part + each),
            )

        sums = block_loop(ref, 1, one, sums)
    return sums


def moments_kernel(rows, *refs):
    refs, out_ref = refs[:4], refs[4]
    zero = jnp.zeros((8, refs[0].shape[-1]), F32)
    out_ref[:8, :], out_ref[8:, :] = moments_of(
        refs, rows, block_at(refs[0], 0, rows)[1], (zero, zero)
    )


def near_moments(lines, rows):
    (sums,) = run(
        functools.partial(moments_kernel, rows), [shape((16, lines[0].shape[-1]))], lines[:4]
    )
    return sums


def moments(refs, sums_ref, rows, node_total):
    pivot = block_at(refs[0], 0, rows)[1]
    sums = moments_of(refs[4:], rows, pivot, (sums_ref[:8, :], sums_ref[8:, :]))
    shift = jnp.sum(sums[0], axis=0, keepdims=True) / node_total
    variance = jnp.sum(sums[1], axis=0, keepdims=True) / node_total - shift * shift
    return pivot + shift, lax.rsqrt(jnp.maximum(variance, 0.0) + EPS_NORM)


def gelu_half(value):
    square = value * value
    bend = jnp.tanh(value * (ROOT + (ROOT * BEND) * square))
    return 0.5 + 0.5 * bend, square


def gelu_slope(value, half, square):
    return half + (value * half) * (1.0 - half) * (2 * ROOT + (6 * ROOT * BEND) * square)


def with_columns(refs, near_ref, far_ref, act, total):
    rows, columns = near_ref.shape
    for n, ref in enumerate(refs):
        adjacent_ref = far_ref if n >= 4 else near_ref

        def one(i, total, ref=ref, adjacent_ref=adjacent_ref, at=n % 4 * (columns // 4)):
            start = at + i * rows
            if not isinstance(start, int):
                start = pl.multiple_of(start, 4 * rows)
            blocks = [block_at(ref, i + j, rows) for j in range(4)]
            return act(blocks, adjacent_ref[:, pl.ds(start, 4 * rows)], total)

        total = block_loop(ref, 4, one, total)
    return total


def split_sums(total):
    high = total.astype(BF).astype(F32)
    low = (total - high).astype(BF).astype(F32)
    return jnp.concatenate([high, low])


def joined(parts):
    parts = parts.astype(F32)
    return parts[: EXTRA // 2] + parts[EXTRA // 2 :]


def put_sums(out_ref, width, parts):
    out_ref[width:, :LANES] = parts.astype(BF)
    if out_ref.shape[1] > LANES:
        out_ref[width:, LANES:] = jnp.zeros((EXTRA, out_ref.shape[1] - LANES), BF)


def pack_into(out_ref, turned, parts):
    width = turned.shape[0]
    out_ref[:width, :] = turned.astype(BF)
    if parts is not None:
        put_sums(out_ref, width, parts)


def add_up(values):
    values = list(values)
    while len(values) > 1:
        values = [values[i] + values[i + 1] for i in range(0, len(values), 2)]
    return values[0]


def cross(turned_refs, level_refs, start, stop, width, out):
    if len(level_refs) == 1:
        count = level_refs[0].shape[0]
        turned = [turned_refs[0].at[i] for i in range(count)]
        levels = [level_refs[0].at[i] for i in range(count)]
    else:
        turned, levels = turned_refs, level_refs
    total = None
    for i in range(0, len(levels), 2):
        left = jnp.concatenate([turned[i][:width, :], turned[i + 1][:width, :]], axis=1)
        right = jnp.concatenate([levels[i][:, start:stop], levels[i + 1][:, start:stop]])
        part = dot(left, right)
        total = part if total is None else total + part
    out(total)


def cross_kernel(width, count, *refs):
    turned_refs, level_refs, (send_ref,) = refs[:count][::-1], refs[count : 2 * count], refs[2 * count :]
    half = send_ref.shape[1]

    def out(value):
        send_ref[:width, :] = value.astype(BF)

    cross(turned_refs, level_refs, half, 2 * half, width, out)
    if send_ref.shape[0] > width:
        if count == 1:
            parts = [joined(turned_refs[0][i, width:, :]) for i in range(turned_refs[0].shape[0])]
        else:
            parts = [joined(ref[width:, :]) for ref in turned_refs]
        put_sums(send_ref, width, split_sums(add_up(parts)))


def keep_kernel(width, count, *refs):
    turned_refs, level_refs, (out_ref,) = refs[:count][::-1], refs[count : 2 * count], refs[2 * count :]

    def out(value):
        out_ref[...] = value

    cross(turned_refs, level_refs, 0, out_ref.shape[1], width, out)


def fold_kernel(kept_ref, send_ref, got_ref, own_ref, *piece_refs):
    width = kept_ref.shape[0]
    for k in range(4):
        cols = slice(k * LANES, (k + 1) * LANES)
        value = kept_ref[:, cols] + got_ref[:width, cols].astype(F32)
        if k == 0:
            own_ref[:width, :] = value
        else:
            piece_refs[k - 1][:width, :] = value.astype(BF)
    if own_ref.shape[0] > width:
        parts = split_sums(joined(send_ref[width:, :LANES]) + joined(got_ref[width:, :LANES]))
        own_ref[width:, :] = parts
        for piece_ref in piece_refs:
            put_sums(piece_ref, width, parts)


def spread_back(packed, levels, width):
    tall = packed.shape[0]
    if short_line():
        turned = [packed] + [pass_line(packed, k) for k in range(1, 4)]
    else:
        turned = [lax.all_gather(packed, "z", axis=0)]
    count = len(levels)
    half = levels[0].shape[-1] // 2
    work = 8 * width * LANES * half
    (send,) = run(
        functools.partial(cross_kernel, width, count),
        [shape((tall, half), BF)],
        [*turned[::-1], *levels],
        flops=work,
    )
    got = swap(send, 1)
    (kept,) = run(
        functools.partial(keep_kernel, width, count),
        [shape((width, half))],
        [*turned[::-1], *levels],
        flops=work,
    )
    own, *pieces = run(
        fold_kernel, [shape((tall, LANES))] + [shape((tall, LANES), BF)] * 3, [kept, send, got]
    )
    return [swap(pieces[k - 1], 2 * k) for k in (3, 2, 1)] + [own]


def line_total(refs, width):
    total = add_up(ref[:width, :].astype(F32) for ref in refs)
    if refs[0].shape[0] == width:
        return total, None
    return total, add_up(joined(ref[width:, :]) for ref in refs)


def wide(sums, row):
    return jnp.concatenate([sums[row : row + 1], sums[row + 1 : row + 2]], axis=1)


def put_wide(ref, row, value):
    ref[row : row + 1, :] = value[:, :LANES]
    ref[row + 1 : row + 2, :] = value[:, LANES:]


def layer_kernel(node_total, layer, near_ref, far_ref, weight_ref, norm_ref, *refs):
    near_sums_ref, refs, (out_ref, stats_ref) = refs[0], refs[1:9], refs[9:]
    rows, width = near_ref.shape[0], refs[0].shape[-1]
    mean_value, inverse = moments(refs, near_sums_ref, rows, node_total)
    stats_ref[0:1, :] = mean_value
    stats_ref[1:2, :] = inverse
    scale = norm_ref[2 * layer : 2 * layer + 1, :] * inverse
    start = norm_ref[2 * layer + 1 : 2 * layer + 2, :] - mean_value * scale
    low = weight_ref[...].astype(BF)

    def act(blocks, adjacent, total):
        hidden = []
        for value, centre in blocks:
            value = value * scale + (start + centre * scale)
            hidden.append((value * gelu_half(value)[0]).astype(BF))
        projected = dot(jnp.concatenate(hidden), low).astype(BF)
        return total + dot(adjacent, projected)

    total = jnp.zeros((rows, low.shape[1]), F32)
    centre_into(out_ref, with_columns(refs, near_ref, far_ref, act, total))


def slopes_kernel(layer, near_ref, far_ref, norm_ref, stats_ref, *refs):
    refs, out_ref = refs[:8], refs[8]
    mean_value, inverse = stats_ref[0:1, :], stats_ref[1:2, :]
    gain = norm_ref[2 * layer : 2 * layer + 1, :]
    offset = norm_ref[2 * layer + 1 : 2 * layer + 2, :]
    out_ref[...] = jnp.zeros(out_ref.shape, F32)

    def act(blocks, adjacent, carry):
        slopes = []
        for value, centre in blocks:
            normed = value * inverse + (centre - mean_value) * inverse
            value = gain * normed + offset
            slope = gelu_slope(value, *gelu_half(value))
            slopes.append(jnp.concatenate([slope.astype(BF), (slope * normed).astype(BF)], axis=1))
        out_ref[...] += dot(adjacent, jnp.concatenate(slopes))
        return carry

    with_columns(refs, near_ref, far_ref, act, 0)


def head_low_of(weight_ref, tall_ref):
    tall_ref[...] = jnp.zeros(tall_ref.shape, F32)
    tall_ref[: weight_ref.shape[0], :] = weight_ref[...]
    return tall_ref[...].astype(BF)


def head_kernel(node_total, near_ref, far_ref, weight_ref, norm_ref, notes_ref, *refs):
    near_sums_ref, refs, rest = refs[0], refs[1:9], refs[9:]
    packed_ref, stats_ref, total_ref, sums_ref, tall_ref = rest
    rows, width = near_ref.shape[0], refs[0].shape[-1]
    classes = weight_ref.shape[0]
    mean_value, inverse = moments(refs, near_sums_ref, rows, node_total)
    stats_ref[0:1, :] = mean_value
    stats_ref[1:2, :] = inverse
    gain, offset = norm_ref[2:3, :], norm_ref[3:4, :]
    low = head_low_of(weight_ref, tall_ref)
    total_ref[...] = jnp.zeros(total_ref.shape, F32)

    def act(blocks, adjacent, carry):
        hidden, slopes = [], []
        for value, centre in blocks:
            normed = value * inverse + (centre - mean_value) * inverse
            value = gain * normed + offset
            half, square = gelu_half(value)
            slope = gelu_slope(value, half, square)
            hidden.append((value * half).astype(BF))
            slopes.append(jnp.concatenate([slope.astype(BF), (slope * normed).astype(BF)], axis=1))
        headed = dot_turned(jnp.concatenate(hidden), low).astype(BF)
        both = jnp.concatenate([headed, jnp.concatenate(slopes)], axis=1)
        total_ref[...] += dot(adjacent, both)
        return carry

    with_columns(refs, near_ref, far_ref, act, 0)

    lane = lax.broadcasted_iota(jnp.int32, (rows, LANES), 1)
    sums_ref[...] = jnp.zeros(sums_ref.shape, F32)
    logits = jnp.where(lane < classes, total_ref[:, :LANES] + notes_ref[2:3, :], -1e30)
    logits = logits - jnp.max(logits, axis=1, keepdims=True)
    raised = jnp.exp(logits)
    whole = jnp.sum(raised, axis=1, keepdims=True)
    label = jnp.broadcast_to(notes_ref[0:1, :], (LANES, rows)).T
    onehot = jnp.where(lane.astype(F32) == label, 1.0, 0.0)
    weight = jnp.broadcast_to(notes_ref[1:2, :], (LANES, rows)).T
    losses = jnp.log(whole) - jnp.sum(onehot * logits, axis=1, keepdims=True)
    d_logits = (raised / whole - onehot) * weight
    d_low = d_logits.astype(BF)
    d_wide = dot(d_low, low)
    put_wide(sums_ref, 0, jnp.sum(d_wide * total_ref[:, LANES : LANES + width], axis=0, keepdims=True))
    put_wide(sums_ref, 2, jnp.sum(d_wide * total_ref[:, LANES + width :], axis=0, keepdims=True))
    sums_ref[4:5, :] = jnp.sum(d_logits, axis=0, keepdims=True)
    sums_ref[5:6, :] = jnp.sum(
        jnp.where(lane == 0, losses * weight, weight), axis=0, keepdims=True
    )
    pack_into(packed_ref, d_logits.T[:HEAD_ROWS], split_sums(sums_ref[...]))


def backward_norm(d_hidden, own_ref, stats_ref, norm_ref, layer, shift_grad, gain_grad, node_total):
    rows = own_ref.shape[0] - EXTRA
    mean_value, inverse = stats_ref[0:1, :], stats_ref[1:2, :]
    gain = norm_ref[2 * layer : 2 * layer + 1, :]
    centre = own_ref[rows:, :].astype(F32)[:1]
    normed = own_ref[:rows, :].astype(F32) * inverse + (centre - mean_value) * inverse
    value = gain * normed + norm_ref[2 * layer + 1 : 2 * layer + 2, :]
    half, square = gelu_half(value)
    d_pre = d_hidden * gelu_slope(value, half, square)
    d_summed = (gain * inverse) * (d_pre - (shift_grad + normed * gain_grad) / node_total)
    return d_summed, value * half


def second_kernel(
    node_total,
    head_ref,
    weight_ref,
    norm_ref,
    summed_ref,
    stats_ref,
    slopes_ref,
    *refs,
):
    refs, (packed_ref, grad_ref, out_ref, sums_ref, tall_ref) = refs[:4], refs[4:]
    headed, sums = line_total(refs, HEAD_ROWS)
    rows = headed.shape[1]
    each = 1.0 / sums[5:6, 1:2]
    headed = headed * each
    put_row = lax.broadcasted_iota(jnp.int32, sums.shape, 0)
    out_ref[...] = jnp.where(put_row == 5, sums, sums * each)
    turned_back = jnp.concatenate([headed, jnp.zeros((LANES - HEAD_ROWS, rows), F32)]).T
    d_hidden = dot(turned_back.astype(BF), head_low_of(head_ref, tall_ref))
    d_summed, hidden = backward_norm(
        d_hidden, summed_ref, stats_ref, norm_ref, 1, wide(sums, 0) * each, wide(sums, 2) * each, node_total
    )
    grad_ref[...] = dot(headed.astype(BF), hidden.astype(BF))
    d_wide = dot_turned(d_summed.astype(BF), weight_ref[...].astype(BF))
    width = d_wide.shape[1]
    put_wide(sums_ref, 0, jnp.sum(d_wide * slopes_ref[:, :width], axis=0, keepdims=True))
    put_wide(sums_ref, 2, jnp.sum(d_wide * slopes_ref[:, width:], axis=0, keepdims=True))
    sums_ref[4:8, :] = jnp.zeros((4, LANES), F32)
    pack_into(packed_ref, d_summed.T, split_sums(sums_ref[...]))


def mix_kernel(near_ref, far_ref, *refs):
    outs = 1 if len(refs) == 2 else 4
    level_refs, out_refs = refs[:outs], refs[outs:]

    def one(level_ref):
        total = None
        for n in range(0, 8, 2):
            ref = far_ref if n >= 4 else near_ref
            left = jnp.concatenate([ref[n % 4], ref[n % 4 + 1]], axis=1)
            part = dot_turned(left, level_ref[:, n * TILE : (n + 2) * TILE])
            total = part if total is None else total + part
        return total

    if outs == 1:

        def step(i, carry):
            out_refs[0][i] = one(level_refs[0].at[i])
            return carry

        lax.fori_loop(0, level_refs[0].shape[0], step, 0)
        return
    for level_ref, out_ref in zip(level_refs, out_refs, strict=True):
        out_ref[...] = one(level_ref).astype(out_ref.dtype)


def first_kernel(node_total, inputs_tall, mixes, weight_ref, norm_ref, summed_ref, stats_ref, head_ref, *refs):
    mix_refs, refs = refs[:mixes], refs[mixes:]
    refs, (away_ref, kept_ref, out_ref, pile_ref) = refs[:4], refs[4:]
    width = weight_ref.shape[1]
    d_projected, sums = line_total(refs, width)
    out_ref[...] = sums
    d_projected = d_projected.T.astype(BF)
    d_hidden = dot_turned(d_projected, weight_ref[...].astype(BF))
    d_summed, hidden = backward_norm(
        d_hidden, summed_ref, stats_ref, norm_ref, 0, wide(sums, 0), wide(sums, 2), node_total
    )
    mixed = add_up(ref[...].astype(F32) for ref in mix_refs).astype(BF)
    pile_ref[...] = jnp.zeros(pile_ref.shape, F32)
    pile_ref[: mixed.shape[0], :] = dot(mixed, d_summed.astype(BF))
    at = inputs_tall
    pile_ref[at : at + width, :] = dot(hidden.T.astype(BF), d_projected)
    at += width
    pile_ref[at : at + HEAD_ROWS, :] = head_ref[...]
    half = away_ref.shape[0]
    core = lax.axis_index("c")
    away_ref[...] = pile_ref[pl.ds(pl.multiple_of((1 - core) * half, half), half), :].astype(BF)
    kept_ref[...] = pile_ref[pl.ds(pl.multiple_of(core * half, half), half), :]


def pile_core_kernel(kept_ref, got_ref, own_ref, *piece_refs):
    size = own_ref.shape[0]
    here = 2 * lax.axis_index("y") + lax.axis_index("x")
    for k in range(4):
        at = pl.ds(pl.multiple_of(jnp.bitwise_xor(here, k) * size, size), size)
        value = kept_ref[at, :] + got_ref[at, :].astype(F32)
        if k == 0:
            own_ref[...] = value
        else:
            piece_refs[k - 1][...] = value.astype(BF)


def pile_sum_kernel(own_ref, *refs):
    parts = [own_ref, *refs[:3]]
    refs[3][...] = add_up(ref[...].astype(F32) for ref in parts).astype(refs[3].dtype)


def update_kernel(inputs_tall, *refs):
    pieces, refs = refs[:8], refs[8:]
    inputs, outs, pile_ref = refs[:9], refs[9:18], refs[18]
    size, width = pieces[0].shape
    here = 2 * lax.axis_index("y") + lax.axis_index("x")
    core = lax.axis_index("c")
    for n, ref in enumerate(pieces):
        at = (jnp.bitwise_xor(core, n // 4) * 4 + jnp.bitwise_xor(here, 3 - n % 4)) * size
        pile_ref[pl.ds(pl.multiple_of(at, size), size), :] = ref[...].astype(F32)
    tall = inputs[0].shape[0]
    grads = (
        pile_ref[:tall, :],
        pile_ref[inputs_tall : inputs_tall + width, :],
        pile_ref[inputs_tall + width : inputs_tall + width + inputs[6].shape[0], :],
    )
    for n in range(3):
        weight, first, second = (ref[...] for ref in inputs[3 * n : 3 * n + 3])
        results = adamw(weight, grads[n], first, second, RATE_MATRIX)
        for ref, value in zip(outs[3 * n : 3 * n + 3], results, strict=True):
            ref[...] = value


def sum_pile(away, kept):
    size = away.shape[0] // 4
    width = away.shape[1]
    got = swap(away, 1)
    own, *pieces = run(
        pile_core_kernel, [shape((size, width))] + [shape((size, width), BF)] * 3, [kept, got]
    )
    got = [swap(pieces[k - 1], 2 * k) for k in range(1, 4)]
    if short_line():
        (shard,) = run(pile_sum_kernel, [shape((size, width), BF)], [own, *got])
        got = [pass_line(shard, k) for k in range(1, 4)]
        (shard,) = run(pile_sum_kernel, [shape((size, width), BF)], [*got[::-1], shard])
    else:
        (shard,) = run(pile_sum_kernel, [shape((size, width))], [own, *got])
        shard = lax.psum(shard, "z").astype(BF)
    pieces = [shard] + [swap(shard, 2 * k) for k in range(1, 4)]
    others = [swap(piece, 1) for piece in pieces]
    return pieces[::-1] + others[::-1]


def first_sum_kernel(near_ref, far_ref, *refs):
    refs, out_ref = refs[:8], refs[8]
    count, rows, width = refs[0].shape
    total = jnp.zeros((rows, width), F32)
    for n, ref in enumerate(refs):
        adjacent_ref = far_ref if n >= 4 else near_ref
        at = n % 4 * count * rows
        total = total + dot(
            adjacent_ref[:, at : at + count * rows], ref[...].reshape(count * rows, width)
        )
    centre_into(out_ref, total)


def per_device(
    features,
    adjacency,
    tile_mask,
    labels,
    train_mask,
    w_first,
    w_second,
    w_head,
    norm_params,
    head_bias,
    m_first,
    m_second,
    m_head,
    m_norms,
    m_bias,
    v_first,
    v_second,
    v_head,
    v_norms,
    v_bias,
):
    rows, node_total = adjacency.shape
    inputs, hidden = w_first.shape
    classes = w_head.shape[1]
    half = node_total // 2
    length = lax.axis_size("z")
    tall = rows + EXTRA
    inputs_tall = -(-inputs // EXTRA) * EXTRA
    head_turned = w_head.T
    work = 2 * rows * node_total * hidden

    if short_line():
        level_shapes = [shape((rows, 8 * rows), BF)] * 4
    else:
        level_shapes = [shape((length, rows, 8 * rows), BF)]
    near, far, notes, *levels = run(
        arrange_kernel,
        [shape((rows, half), BF)] * 2 + [shape((8, LANES))] + level_shapes,
        [tile_mask, adjacency, labels[None], train_mask[None], head_bias[None]],
        scalars=1,
    )

    projected = dot(features, w_first.astype(BF)).astype(BF)
    turned = features.T
    short = short_line()
    if not short:
        levels = [lax.all_to_all(levels[0], "z", 0, 0)]
    around, passed, unused, (turned_x,) = gather_all(
        projected,
        [(levels[1], 1), (levels[2], 2)] if short else (),
        centred=False,
        early=[swap(turned, 2)],
        tied=False,
    )
    turned = jnp.stack([turned, turned_x])
    turned = jnp.concatenate([turned, swap(turned, 4)])
    if short:
        levels[1:3] = passed
    (summed_one,) = run(
        first_sum_kernel, [shape((tall, hidden), BF)], [near, far, *around], flops=work
    )
    around, passed, *unused = gather_all(summed_one, [(levels[3], 3)] if short else ())
    if short:
        levels[3:] = passed
    summed_two, stats_one = run(
        functools.partial(layer_kernel, node_total, 0),
        [shape((tall, hidden), BF), shape((8, hidden))],
        [near, far, w_second, norm_params, near_moments(around, rows), *around],
        flops=3 * work,
    )
    (slopes_one,) = run(
        functools.partial(slopes_kernel, 0),
        [shape((rows, 2 * hidden))],
        [near, far, norm_params, stats_one, *around],
        flops=3 * work,
    )
    if short:
        mixed_shapes = [shape((inputs, rows))] + [shape((inputs, rows), BF)] * 3
    else:
        mixed_shapes = [shape((length, inputs, rows))]
    mixed = run(
        mix_kernel, mixed_shapes, [turned, swap(turned, 1), *levels], flops=2 * work
    )
    around, passed, (slopes_one,), unused = gather_all(
        summed_two, [(mixed[k], k) for k in (1, 2, 3)] if short else (), [slopes_one]
    )
    if short:
        mixed = [mixed[0], *passed]
    else:
        mixed = [lax.psum_scatter(mixed[0], "z", scatter_dimension=0)]
    packed, stats_two = run(
        functools.partial(head_kernel, node_total),
        [shape((HEAD_ROWS + EXTRA, rows), BF), shape((8, hidden))],
        [
            near,
            far,
            head_turned,
            norm_params,
            notes,
            near_moments(around, rows),
            *around,
        ],
        scratch=[
            pltpu.VMEM((rows, LANES + 2 * hidden), F32),
            pltpu.VMEM((8, LANES), F32),
            pltpu.VMEM((LANES, hidden), F32),
        ],
        flops=4 * work,
    )

    packed, head_grad, sums_two = run(
        functools.partial(second_kernel, node_total),
        [shape((hidden + EXTRA, rows), BF), shape((HEAD_ROWS, hidden)), shape((8, LANES))],
        [
            head_turned,
            w_second,
            norm_params,
            summed_two,
            stats_two,
            slopes_one,
            *spread_back(packed, levels, HEAD_ROWS),
        ],
        scratch=[pltpu.VMEM((8, LANES), F32), pltpu.VMEM((LANES, hidden), F32)],
        flops=work // 4,
    )
    size = -(-(inputs_tall + hidden + HEAD_ROWS) // (8 * EXTRA)) * EXTRA
    away, kept, sums_one = run(
        functools.partial(first_kernel, node_total, inputs_tall, len(mixed)),
        [shape((4 * size, hidden), BF), shape((4 * size, hidden)), shape((8, LANES))],
        [
            w_second,
            norm_params,
            summed_one,
            stats_one,
            head_grad,
            *mixed,
            *spread_back(packed, levels, hidden),
        ],
        scratch=[pltpu.VMEM((8 * size, hidden), F32)],
        flops=work,
    )
    matrices = (
        *(w_first, m_first, v_first, w_second, m_second, v_second),
        *(head_turned, m_head.T, v_head.T),
    )
    updated = run(
        functools.partial(update_kernel, inputs_tall),
        [shape(block.shape) for block in matrices],
        [*sum_pile(away, kept), *matrices],
        scratch=[pltpu.VMEM((8 * size, hidden), F32)],
    )
    updated = [*updated[:6], *(block.T for block in updated[6:])]

    def pair(sums):
        return sums[2:4].reshape(1, hidden), sums[0:2].reshape(1, hidden)

    norm_grad = jnp.concatenate([*pair(sums_one), *pair(sums_two)])
    norms = adamw(norm_params, norm_grad, m_norms, v_norms, RATE_SMALL)
    bias = adamw(head_bias, sums_two[4, :classes], m_bias, v_bias, RATE_SMALL)
    loss_sum, train_count = sums_two[5, 0], sums_two[5, 1]
    return (
        loss_sum,
        train_count,
        *(
            part
            for n in range(3)
            for part in (updated[n], updated[3 + n], updated[6 + n], norms[n], bias[n])
        ),
    )


def solution(mesh):
    wide_mesh = Mesh(mesh.devices.reshape(-1, 2, 2, 2), EVERY)
    split = (P(EVERY, None),) * 3 + (P(EVERY),) * 2
    return jax.shard_map(
        per_device,
        mesh=wide_mesh,
        in_specs=split + (P(),) * 15,
        out_specs=(P(),) * 17,
        check_vma=False,
    )
```
